1024 devices in a mesh: expert: 32 (over y, x, core), dp: 32 (over z).
Axes of the slice: x: 4, y: 4, z: 32, core: 2. Of those that a mesh axis runs over, the one named last changes fastest.
Arguments:
- tokens: bfloat16 [32768, 1024], P(('expert', 'dp')), may hold values from -6 to 6
- expert_ids: int32 [32768, 8], P(('expert', 'dp')), may hold values from 0 to 63, all different within a row; in each aligned block of 32 rows (0 to 31, 32 to 63, ...) at most 8 rows name the same one
- gate_probs: float32 [32768, 8], P(('expert', 'dp')), may hold values from 0.05 to 0.4
- w_gate: bfloat16 [64, 1024, 384], P('expert'), may hold values from -0.1875 to 0.1875
- w_up: bfloat16 [64, 1024, 384], P('expert'), may hold values from -0.1875 to 0.1875
- w_down: bfloat16 [64, 384, 1024], P('expert'), may hold values from -0.3125 to 0.3125
- out_grad: bfloat16 [32768, 1024], P(('expert', 'dp')), may hold values from -24 to 24
Outputs:
- mixed: bfloat16 [32768, 1024], P(('expert', 'dp'))
- token_grad: bfloat16 [32768, 1024], P(('expert', 'dp'))
- down_grad: float32 [64, 384, 1024], P('expert', None, 'dp')
The draws below stay inside these ranges and needn't reach their ends.
Inputs may be any that keep to these rules, and one draw needn't show every extreme that they name: `expert_ids`: in each aligned block of 32 rows (the rows of one device) no expert is named by more than 8 rows, a bound that some block reaches; the 8 experts of a row differ.
All inputs are finite; a program needn't handle non-finite values.
Results may differ from the reference program's by a relative error of at most 0.02.
Values may be sent and summed in bfloat16 or wider, within the bound.
A program may use at most 64 MiB of HBM per device.

```python
import math
import jax
import jax.numpy as jnp
import numpy as np
from jax import lax

D = 1024
H = 384
TOP = 8
TOK_DEV = 32
EXPERTS = 64
CAP = 8
TOKENS = 32768
N_EXPERT = 32
N_DP = 32


def raised(entries, key, source, target, shards_of, factor):
    def block_of(axis_at):
        return (jnp.arange(entries.shape[axis_at]) // (entries.shape[axis_at] // shards_of)).reshape((-1,) + (1,) * (entries.ndim - 1 - axis_at))

    first = jax.random.permutation(key, shards_of)[block_of(target)]
    far = (block_of(target) + shards_of // 2) % shards_of
    return jnp.where((block_of(source) == first) | (block_of(source) == far), factor * entries, entries)


def block_scale(stream_key, shape, pieces, least, top_value):
    factor_of, own = 1.0, jax.random.fold_in(stream_key, 6)
    for axis_at, shards_of in pieces:
        heights = jnp.exp(jax.random.uniform(jax.random.fold_in(own, axis_at), (shards_of,), jnp.float32, least / len(pieces), top_value / len(pieces)))
        factor_of = factor_of * jnp.repeat(heights, shape[axis_at] // shards_of).reshape([-1 if axis == axis_at else 1 for axis in range(len(shape))])
    return factor_of


def routed_block(key, own, number, rows, count, top, bound, lean):
    ranking = jax.random.permutation(key, count)
    heavy_load, usual = load_shares(count, rows * top, bound, lean, True), load_shares(count, rows * top, bound, lean, False)
    places = jnp.arange(count)

    def named(tallies, turn):
        used = int((tallies > 0).sum())
        fixed = max(1, used // 4)
        passed = fixed + (places - fixed + turn * (used - fixed)) % max(1, count - fixed)
        return jnp.zeros((count,), jnp.int32).at[ranking[jnp.where(places < fixed, places, passed)]].set(jnp.asarray(tallies, jnp.int32))

    tallies = jnp.where(number % 4 == 0, named(heavy_load, number // 4), named(usual, number - number // 4 - 1))
    mixed = jax.random.permutation(jax.random.fold_in(own, 3), count)
    donor, sink = mixed[0:count // 2 * 2:2], mixed[1:count // 2 * 2:2]
    room = jnp.minimum(tallies[donor] - 1, bound - tallies[sink]) // 2
    room = jnp.where((donor == ranking[0]) | (sink == ranking[0]) | (tallies[sink] == 0), 0, jnp.maximum(room, 0))
    passed = jax.random.randint(jax.random.fold_in(own, 4), (count // 2,), 0, 1 << 20) % (room + 1)
    tallies = tallies.at[donor].add(-passed).at[sink].add(passed)
    items = jnp.searchsorted(jnp.cumsum(tallies), jnp.arange(rows * top), side="right").astype(jnp.int32)
    listing = items.reshape(top, rows).T
    listing = listing[jax.random.permutation(jax.random.fold_in(own, 1), rows)]
    turn = jax.random.randint(jax.random.fold_in(own, 2), (rows, 1), 0, top)
    return jnp.take_along_axis(listing, (jnp.arange(top)[None, :] + turn) % top, axis=1)


def load_shares(number_of, total, reach, lean, full):
    portions = [(1 << 20) // math.isqrt(rank ** lean) + 1 for rank in range(1, number_of + 1)]
    largest = reach if full else min(reach, max(-(-total // number_of), total * portions[0] // sum(portions)))
    least = 1 if total - largest >= number_of - 1 else 0
    given, surplus = [largest] + [least] * (number_of - 1), total - largest - least * (number_of - 1)
    while surplus > 0:
        candidates = [i for i in range(1, number_of) if given[i] < largest] or [i for i in range(1, number_of) if given[i] < reach]
        pool, remaining = sum([portions[i] for i in candidates]), surplus
        for i in candidates:
            addition = min(reach - given[i], max(1, remaining * portions[i] // pool), surplus)
            given[i] = given[i] + addition
            surplus = surplus - addition
    return np.array(given)


def centred(stream_key, shape, deviation, bound, split=(), held_as=jnp.bfloat16):
    entries = deviation * jax.random.normal(stream_key, shape, jnp.float32)
    if split:
        entries = entries * block_scale(stream_key, shape, split, -0.22, 0.18)
    return jnp.clip(entries, -bound, bound).astype(held_as)


def bell_draw_with(own_key, dims, spread, limit, split, heavy, held_as=jnp.bfloat16):
    array = spread * jax.random.normal(own_key, dims, jnp.float32)
    if split:
        array = array * block_scale(own_key, dims, split, -0.22, 0.18)
    return jnp.clip(raised(array, jax.random.fold_in(own_key, 3), *heavy), -limit, limit).astype(held_as)


def setup_inputs(seed: int = 0) -> dict:
    key_of = jax.random.split(jax.random.key(seed), 8)
    tokens = centred(key_of[0], (TOKENS, D), 1.0, 6.0, ((0, 1024),))
    expert_ids_keys = jax.random.split(jax.random.fold_in(key_of[1], 1), TOKENS // TOK_DEV)
    expert_ids_turns = jax.random.permutation(jax.random.fold_in(key_of[1], 3), TOKENS // TOK_DEV)
    expert_ids = jax.vmap(lambda own, number: routed_block(jax.random.fold_in(key_of[1], 2), own, number, TOK_DEV, EXPERTS, TOP, CAP, 2))(expert_ids_keys, expert_ids_turns).reshape((TOKENS, TOP))
    gate_probs = jnp.clip(0.05 + 0.35 * jax.random.uniform(key_of[2], (TOKENS, TOP), jnp.float32) ** block_scale(key_of[2], (TOKENS, TOP), ((0, 1024),), -0.2, 0.2), 0.05, 0.4)
    w_gate = centred(key_of[3], (EXPERTS, D, H), D ** -0.5, 0.1875, ((0, 32),))
    w_up = centred(key_of[4], (EXPERTS, D, H), D ** -0.5, 0.1875, ((0, 32),))
    w_down = centred(key_of[5], (EXPERTS, H, D), H ** -0.5, 0.3125, ((0, 32),))
    out_grad = bell_draw_with(key_of[6], (TOKENS, D), 1.0, 24.0, ((0, 1024),), (0, 1, 1024, 6.0))
    return dict(tokens=tokens, expert_ids=expert_ids, gate_probs=gate_probs, w_gate=w_gate, w_up=w_up, w_down=w_down, out_grad=out_grad)


def reference(tokens, expert_ids, gate_probs, w_gate, w_up, w_down, out_grad):
    rows_all = TOKENS * TOP
    flat = expert_ids.reshape(-1).astype(jnp.int32)
    row_tok = (jnp.arange(rows_all, dtype=jnp.int32) // TOP).astype(jnp.int32)
    group = ((row_tok // TOK_DEV) % N_DP).astype(jnp.int32)
    keys = (flat * N_DP + group).astype(jnp.int32)
    order = jnp.argsort(keys, stable=True).astype(jnp.int32)
    sorted_keys = keys[order]
    segs = jnp.arange(EXPERTS * N_DP, dtype=jnp.int32)
    starts = jnp.searchsorted(sorted_keys, segs, side="left").astype(jnp.int32)
    ends = jnp.searchsorted(sorted_keys, segs, side="right").astype(jnp.int32)
    maxrows = CAP * N_EXPERT
    order_pad = jnp.concatenate([order, jnp.full((maxrows,), rows_all, jnp.int32)])
    x_pad = jnp.concatenate([tokens, jnp.zeros((1, D), tokens.dtype)], 0)
    c_pad = jnp.concatenate([out_grad, jnp.zeros((1, D), out_grad.dtype)], 0).astype(jnp.float32)
    p_pad = jnp.concatenate([gate_probs.reshape(-1), jnp.zeros((1,), gate_probs.dtype)]).astype(jnp.float32)

    def step(carry, seg):
        mix_acc, grad_acc, down_acc = carry
        expert = (seg // N_DP).astype(jnp.int32)
        idx = lax.dynamic_slice_in_dim(order_pad, starts[seg], maxrows)
        valid = jnp.arange(maxrows, dtype=jnp.int32) < (ends[seg] - starts[seg])
        idx = jnp.where(valid, idx, rows_all).astype(jnp.int32)
        tok = (idx // TOP).astype(jnp.int32)
        wg = w_gate[expert]
        wu = w_up[expert]
        wd = w_down[expert]
        xr = x_pad[tok]
        prob = p_pad[idx][:, None]
        gate_act = jnp.dot(xr, wg, preferred_element_type=jnp.float32)
        up_act = jnp.dot(xr, wu, preferred_element_type=jnp.float32)
        sig = jax.nn.sigmoid(gate_act)
        hidden = (gate_act * sig * up_act).astype(jnp.bfloat16)
        out = jnp.dot(hidden, wd, preferred_element_type=jnp.float32).astype(jnp.bfloat16)
        row_grad = (prob * c_pad[tok]).astype(jnp.bfloat16)
        hidden_grad = jnp.dot(row_grad, wd.T, preferred_element_type=jnp.float32)
        partial_value = jnp.dot(hidden.T, row_grad, preferred_element_type=jnp.float32).astype(jnp.bfloat16)
        gate_grad = (hidden_grad * up_act * sig * (1.0 + gate_act * (1.0 - sig))).astype(jnp.bfloat16)
        up_grad = (hidden_grad * gate_act * sig).astype(jnp.bfloat16)
        input_grad = (jnp.dot(gate_grad, wg.T, preferred_element_type=jnp.float32)
                      + jnp.dot(up_grad, wu.T, preferred_element_type=jnp.float32)).astype(jnp.bfloat16)
        mix_acc = mix_acc.at[tok].add(prob * out.astype(jnp.float32))
        grad_acc = grad_acc.at[tok].add(input_grad.astype(jnp.float32))
        down_acc = down_acc.at[expert].add(partial_value.astype(jnp.float32))
        return (mix_acc, grad_acc, down_acc), None

    init = (jnp.zeros((TOKENS + 1, D), jnp.float32), jnp.zeros((TOKENS + 1, D), jnp.float32),
            jnp.zeros((EXPERTS, H, D), jnp.float32))
    (mix_acc, grad_acc, down_acc), _ = lax.scan(step, init, segs)
    mixed = mix_acc[:TOKENS].astype(jnp.bfloat16)
    token_grad = grad_acc[:TOKENS].astype(jnp.bfloat16)
    return mixed, token_grad, down_acc
```

```python
import jax
import jax.numpy as jnp
from jax import lax
from jax.experimental import pallas as pl
from jax.experimental.pallas import tpu as pltpu
from jax.sharding import PartitionSpec as P

MESH = pl.DeviceIdType.MESH


def ring_kernel(n, p_ref, out_ref, sa, ra, sb, rb, sa_sem, ra_sem, sb_sem, rb_sem):
    me = lax.axis_index("dp")
    right, left = lax.rem(me + 1, n), lax.rem(me + n - 1, n)
    half = n // 2
    subs, _, cols = out_ref.shape
    share = out_ref.shape[1]

    def chunk(dest, sub):
        return p_ref[
            pl.ds(pl.multiple_of(dest * share, share), share), sub * cols : (sub + 1) * cols
        ].astype(jnp.float32)

    def up(step, sub):
        return pltpu.make_async_remote_copy(
            src_ref=sa.at[step, sub],
            dst_ref=ra.at[step, sub],
            send_sem=sa_sem.at[step, sub],
            recv_sem=ra_sem.at[step, sub],
            device_id={"dp": right},
            device_id_type=MESH,
        )

    def down(step, sub):
        return pltpu.make_async_remote_copy(
            src_ref=sb.at[step, sub],
            dst_ref=rb.at[step, sub],
            send_sem=sb_sem.at[step, sub],
            recv_sem=rb_sem.at[step, sub],
            device_id={"dp": left},
            device_id_type=MESH,
        )

    barrier = pltpu.get_barrier_semaphore()
    for neighbour in (left, right):
        pl.semaphore_signal(barrier, inc=1, device_id={"dp": neighbour}, device_id_type=MESH)
    pl.semaphore_wait(barrier, 2)

    def up_dest(step):
        return lax.rem(me + half - step, n)

    def down_dest(step):
        return lax.rem(me + n - (half - 1) + step, n)

    for sub in range(subs):
        sa[0, sub] = chunk(up_dest(0), sub).astype(sa.dtype)
        up(0, sub).start()
        sb[0, sub] = chunk(down_dest(0), sub).astype(sb.dtype)
        down(0, sub).start()

    def step(s, carry):
        for sub in range(subs):
            up(s - 1, sub).wait_recv()
            sa[s, sub] = (ra[s - 1, sub].astype(jnp.float32) + chunk(up_dest(s), sub)).astype(sa.dtype)
            up(s, sub).start()
            down(s - 1, sub).wait_recv()
            sb[s, sub] = (rb[s - 1, sub].astype(jnp.float32) + chunk(down_dest(s), sub)).astype(sb.dtype)
            down(s, sub).start()
        return carry

    lax.fori_loop(1, half - 1, step, 0)
    last = half - 1
    for sub in range(subs):
        up(last - 1, sub).wait_recv()
        sa[last, sub] = (ra[last - 1, sub].astype(jnp.float32) + chunk(up_dest(last), sub)).astype(sa.dtype)
        up(last, sub).start()
    for sub in range(subs):
        down(last - 1, sub).wait_recv()
        up(last, sub).wait_recv()
        out_ref[sub] = (
            chunk(me, sub)
            + ra[last, sub].astype(jnp.float32)
            + rb[last - 1, sub].astype(jnp.float32)
        )

    def drain(s, carry):
        for sub in range(subs):
            up(s, sub).wait_send()
            down(s, sub).wait_send()
        return carry

    lax.fori_loop(0, half - 1, drain, 0)
    for sub in range(subs):
        up(last, sub).wait_send()


def ring_sum(partial, n, subs):
    width, cols = partial.shape
    share = width // n
    half = n // 2
    slots = pltpu.VMEM((half, subs, share, cols // subs), jnp.bfloat16)
    fewer = pltpu.VMEM((half - 1, subs, share, cols // subs), jnp.bfloat16)
    sems = pltpu.SemaphoreType.DMA((half, subs))
    return pl.pallas_call(
        lambda *refs: ring_kernel(n, *refs),
        out_shape=jax.ShapeDtypeStruct((subs, share, cols // subs), jnp.float32),
        in_specs=[pl.BlockSpec(memory_space=pltpu.VMEM)],
        out_specs=pl.BlockSpec(memory_space=pltpu.VMEM),
        scratch_shapes=[slots, slots, fewer, fewer, sems, sems, sems, sems],
        compiler_params=pltpu.CompilerParams(
            collective_id=0, has_side_effects=True, vmem_limit_bytes=32 * 1024 * 1024
        ),
    )(partial)


def on_device(tokens, expert_ids, gate_probs, w_gate, w_up, w_down, out_grad):
    tok_dev, top = expert_ids.shape
    width = tokens.shape[1]
    exp_dev = w_gate.shape[0]
    hidden_units = w_gate.shape[2]
    groups = lax.axis_size("expert")
    experts = exp_dev * groups
    capacity = 2 * tok_dev * top // experts
    flat = expert_ids.reshape(-1)
    onehot = (flat[:, None] == jnp.arange(experts, dtype=jnp.int32)[None, :]).astype(jnp.int32)
    slot = jnp.sum((jnp.cumsum(onehot, 0) - 1) * onehot, 1)
    owner = flat // exp_dev
    local = flat % exp_dev
    position = local * (groups * capacity) + owner * capacity + slot
    row_tok = jnp.arange(tok_dev * top, dtype=jnp.int32) // top
    total_slots = exp_dev * groups * capacity
    probs = gate_probs.reshape(-1)[:, None]

    def place(rows):
        buffer = jnp.zeros((total_slots, width), jnp.bfloat16).at[position].set(rows)
        return buffer.reshape(exp_dev, groups, capacity, width)

    send_x = place(tokens[row_tok])
    send_dy = place((probs * out_grad.astype(jnp.float32)[row_tok]).astype(jnp.bfloat16))
    recv_x = lax.all_to_all(send_x, "expert", split_axis=1, concat_axis=1, tiled=True)
    recv_dy = None
    xin = recv_x.reshape(exp_dev, groups * capacity, width)
    gate_act = jnp.einsum("erd,edh->erh", xin, w_gate, preferred_element_type=jnp.float32)
    up_act = jnp.einsum("erd,edh->erh", xin, w_up, preferred_element_type=jnp.float32)
    sigma = jax.nn.sigmoid(gate_act)
    hidden = (gate_act * sigma * up_act).astype(jnp.bfloat16)
    outputs = jnp.einsum("erh,ehd->erd", hidden, w_down, preferred_element_type=jnp.float32).astype(
        jnp.bfloat16
    )
    returned = lax.all_to_all(
        outputs.reshape(exp_dev, groups, capacity, width),
        "expert",
        split_axis=1,
        concat_axis=1,
        tiled=True,
    )
    out_rows = returned.reshape(total_slots, width)[position].astype(jnp.float32)
    mixed = jnp.sum((probs * out_rows).reshape(tok_dev, top, width), 1).astype(jnp.bfloat16)
    recv_dy = lax.all_to_all(send_dy, "expert", split_axis=1, concat_axis=1, tiled=True)
    dyin = recv_dy.reshape(exp_dev, groups * capacity, width)
    hidden_grad = jnp.einsum("erd,ehd->erh", dyin, w_down, preferred_element_type=jnp.float32)
    partial_value = jnp.concatenate(
        [
            jnp.einsum("rd,rh->dh", dyin[e], hidden[e], preferred_element_type=jnp.float32).astype(
                jnp.bfloat16
            )
            for e in range(exp_dev)
        ],
        axis=1,
    )
    down_grad = jnp.transpose(
        ring_sum(partial_value, lax.axis_size("dp"), exp_dev), (0, 2, 1)
    )
    gate_grad = (hidden_grad * up_act * sigma * (1.0 + gate_act * (1.0 - sigma))).astype(
        jnp.bfloat16
    )
    up_grad = (hidden_grad * gate_act * sigma).astype(jnp.bfloat16)
    input_grad = (
        jnp.einsum("erh,edh->erd", gate_grad, w_gate, preferred_element_type=jnp.float32)
        + jnp.einsum("erh,edh->erd", up_grad, w_up, preferred_element_type=jnp.float32)
    ).astype(jnp.bfloat16)
    back = lax.all_to_all(
        input_grad.reshape(exp_dev, groups, capacity, width),
        "expert",
        split_axis=1,
        concat_axis=1,
        tiled=True,
    )
    grad_rows = back.reshape(total_slots, width)[position].astype(jnp.float32)
    token_grad = jnp.sum(grad_rows.reshape(tok_dev, top, width), 1).astype(jnp.bfloat16)
    return (mixed, token_grad, down_grad)


def solution(mesh):
    return jax.shard_map(
        on_device,
        mesh=mesh,
        in_specs=(
            P(("expert", "dp"), None),
            P(("expert", "dp"), None),
            P(("expert", "dp"), None),
            P("expert", None, None),
            P("expert", None, None),
            P("expert", None, None),
            P(("expert", "dp"), None),
        ),
        out_specs=(P(("expert", "dp"), None), P(("expert", "dp"), None), P("expert", None, "dp")),
        check_vma=False,
    )
```

```python
import jax
import jax.numpy as jnp
from jax import lax
from jax.experimental import pallas as pl
from jax.experimental.pallas import tpu as pltpu
from jax.sharding import PartitionSpec as P

MESH = pl.DeviceIdType.MESH
F32 = jnp.float32
BF16 = jnp.bfloat16
SIDE = 4
CHIPS = SIDE * SIDE
TILE = 256

PARENT = {1: 2, 2: 3, 3: 0, 4: 3, 5: 4, 6: 7, 7: 8, 8: 3, 9: 8, 10: 9, 11: 12, 12: 13, 13: 8, 14: 13, 15: 14, 16: 14}
NEXT = dict(PARENT)
NEXT.update({-far: -near for far, near in PARENT.items() if far < 16})
FROM = {near: [far for far in NEXT if NEXT[far] == near] for near in set(NEXT.values())}
LEAVES = [far for far in (16, 15, -15, 11, -11, 10, -10, 6, -6, 5, -5, 1, -1)]


def dot(a, b):
    return lax.dot_general(a, b, (((1,), (0,)), ((), ())), preferred_element_type=F32)


def dot_nt(a, b):
    return lax.dot_general(a, b, (((1,), (1,)), ((), ())), preferred_element_type=F32)


def dot_tn(a, b):
    return lax.dot_general(a, b, (((0,), (0,)), ((), ())), preferred_element_type=F32)


def layer_kernel(
    n_dp,
    tok_hbm, ids_hbm, prob_hbm, wg_hbm, wu_hbm, wd_hbm, grad_hbm,
    mixed_ref, tgrad_ref, down_ref,
    ids_ref, prob_ref, x_all, dy_all, wg, wu, wd, coef_g, coef_u, ph, con_m, con_t, pair_m, pair_t, row_m, row_t, col_m, col_t, part, ring,
    own_sem, w_sem, ag_send, ag_recv, in_send, in_recv, pair_send, pair_recv, row_send, row_recv, col_send, col_recv, z_send, z_recv,
):
    e = lax.axis_index("expert")
    z = lax.axis_index("dp")
    rows, width = tok_hbm.shape
    half = CHIPS * rows
    hid = wg_hbm.shape[2]
    share = width // n_dp
    c = lax.rem(e, 2)
    x = lax.rem(lax.div(e, 2), SIDE)
    y = lax.div(e, 2 * SIDE)
    p = x + c * (y - x)
    q = y + c * (x - y)
    other = e + 1 - 2 * c

    def peer(dp, dq):
        p2, q2 = lax.rem(p + dp, SIDE), lax.rem(q + dq, SIDE)
        x2, y2 = p2 + c * (q2 - p2), q2 + c * (p2 - q2)
        return (y2 * SIDE + x2) * 2 + c

    def block(rp, rq):
        slot = lax.rem(q + SIDE - rq, SIDE) * SIDE + lax.rem(p + SIDE - rp, SIDE)
        return pl.multiple_of(slot * rows, rows)

    mine = block(0, 0)
    own = [
        pltpu.make_async_copy(ids_hbm, ids_ref, own_sem.at[0]),
        pltpu.make_async_copy(prob_hbm, prob_ref, own_sem.at[1]),
        pltpu.make_async_copy(tok_hbm, x_all.at[pl.ds(mine, rows), :width], own_sem.at[2]),
        pltpu.make_async_copy(grad_hbm, dy_all.at[pl.ds(mine, rows), :], own_sem.at[3]),
    ]
    for load in own:
        load.start()

    loads = []
    for k, (src, dst) in enumerate(((wg_hbm, wg), (wu_hbm, wu), (wd_hbm, wd))):
        for i in range(2):
            place = dst.at[i * hid : (i + 1) * hid, :] if k == 2 else dst.at[:, i * hid : (i + 1) * hid]
            load = pltpu.make_async_copy(src.at[i], place, w_sem.at[k, i])
            load.start()
            loads.append(load)

    barrier = pltpu.get_barrier_semaphore()
    near = [{"expert": other}]
    for r in range(1, SIDE):
        near.append({"expert": peer(r, 0)})
        near.append({"expert": peer(0, r)})
    reach = sorted({NEXT[far] - far for far in NEXT})
    for r in reach:
        near.append({"dp": lax.rem(z + n_dp - r, n_dp)})
    for device in near:
        pl.semaphore_signal(barrier, inc=1, device_id=device, device_id_type=MESH)

    experts = x_all.shape[1] - width
    experts //= 2
    expert_of = lax.broadcasted_iota(jnp.int32, (experts, rows), 0)
    gates = jnp.zeros((experts, rows), F32)
    own[0].wait()
    own[1].wait()
    for k in range(ids_ref.shape[0]):
        gates = gates + jnp.where(ids_ref[k : k + 1, :] == expert_of, prob_ref[k : k + 1, :], 0.0)
    high = gates.astype(BF16)
    low = (gates - high.astype(F32)).astype(BF16)
    line = lax.broadcasted_iota(jnp.int32, (experts, 2 * experts), 0)
    lane = lax.broadcasted_iota(jnp.int32, (experts, 2 * experts), 1)
    spread = dot_tn(high, (line == lane).astype(BF16)) + dot_tn(low, (line + experts == lane).astype(BF16))
    x_all[pl.ds(mine, rows), width:] = spread.astype(BF16)
    own[2].wait()
    own[3].wait()

    arrays = (x_all, dy_all)

    def gather(t, rp, rq):
        at = block(0, 0) if rq == 0 else block(rp, 0)
        ref = arrays[t].at[pl.ds(at, rows), :]
        return pltpu.make_async_remote_copy(
            src_ref=ref,
            dst_ref=ref,
            send_sem=ag_send.at[t, rp, rq],
            recv_sem=ag_recv.at[t, rp, rq],
            device_id={"expert": peer(rp, 0) if rq == 0 else peer(0, rq)},
            device_id_type=MESH,
        )

    def cross(t, rp, rq):
        at = block(rp, rq)
        return pltpu.make_async_remote_copy(
            src_ref=arrays[t].at[pl.ds(at, rows), :],
            dst_ref=arrays[t].at[pl.ds(pl.multiple_of(half + at, rows), rows), :],
            send_sem=in_send.at[t, rp, rq],
            recv_sem=in_recv.at[t, rp, rq],
            device_id={"expert": other},
            device_id_type=MESH,
        )

    pl.semaphore_wait(barrier, len(near))

    for t in range(2):
        for r in range(1, SIDE):
            gather(t, r, 0).start()
        for r in range(1, SIDE):
            gather(t, 0, r).start()
        cross(t, 0, 0).start()
    for t in range(2):
        for rp in (1, 3, 2):
            gather(t, rp, 0).wait_recv()
            for rq in range(1, SIDE):
                gather(t, rp, rq).start()
            cross(t, rp, 0).start()

    def pass_on(t):
        for rp in range(SIDE):
            for rq in range(1, SIDE):
                gather(t, rp, rq).wait_recv()
                cross(t, rp, rq).start()

    row_of = lax.broadcasted_iota(jnp.int32, (2 * experts, 2 * hid), 0)
    row_of = jnp.where(row_of >= experts, row_of - experts, row_of)
    col_of = lax.broadcasted_iota(jnp.int32, (2 * experts, 2 * hid), 1)
    pick = (row_of == jnp.where(col_of >= hid, 2 * e + 1, 2 * e)).astype(BF16)

    def forward(i, carry):
        at = pl.ds(pl.multiple_of(i * TILE, TILE), TILE)
        gate = dot(x_all[at, :width], wg[...])
        up = dot(x_all[at, :width], wu[...])
        prob = dot(x_all[at, width:], pick)
        sig = jax.nn.sigmoid(gate)
        act = gate * sig
        scaled = prob * act
        ph[at, :] = (scaled * up).astype(BF16)
        coef_u[at, :] = scaled
        coef_g[at, :] = prob * up * sig * (1.0 + gate * (1.0 - sig))
        return carry

    tiles = half // TILE
    pass_on(0)
    for load in loads[:4]:
        load.wait()
    lax.fori_loop(0, tiles, forward, 0)
    pass_on(1)
    for rp in range(SIDE):
        for rq in range(SIDE):
            cross(0, rp, rq).wait_recv()
    lax.fori_loop(tiles, 2 * tiles, forward, 0)
    for rp in range(SIDE):
        for rq in range(SIDE):
            cross(1, rp, rq).wait_recv()

    def partial(i, carry):
        at = pl.ds(pl.multiple_of(i * 128, 128), 128)
        part[at, :] = dot_tn(dy_all[:, at], ph[...]).astype(BF16)
        return carry

    lax.fori_loop(0, width // 128, partial, 0)

    def owned(far):
        owner = lax.rem(z + n_dp - far, n_dp)
        return pl.ds(pl.multiple_of(owner * share, share), share)

    def travel(far):
        src = ring.at[slot_of[FROM[far][0]]] if far in FROM else part.at[owned(far), :]
        return pltpu.make_async_remote_copy(
            src_ref=src,
            dst_ref=ring.at[slot_of[far]],
            send_sem=z_send.at[slot_of[far]],
            recv_sem=z_recv.at[slot_of[far]],
            device_id={"dp": lax.rem(z + n_dp + NEXT[far] - far, n_dp)},
            device_id_type=MESH,
        )

    slot_of = {far: k for k, far in enumerate(sorted(NEXT))}

    def add_up(far):
        total = part[owned(far), :].astype(F32)
        for child in FROM[far]:
            travel(child).wait_recv()
            total = total + ring[slot_of[child]].astype(F32)
        return total

    def relay(*fars):
        for far in fars:
            ring[slot_of[FROM[far][0]]] = add_up(far).astype(BF16)
            travel(far).start()

    for far in LEAVES:
        travel(far).start()

    def outputs(i, carry):
        at = pl.ds(pl.multiple_of(i * TILE, TILE), TILE)
        con_m[at, :] = dot(ph[at, :], wd[...]).astype(BF16)
        return carry

    def backward(i, carry):
        at = pl.ds(pl.multiple_of(i * TILE, TILE), TILE)
        hidden_grad = dot_nt(dy_all[at, :], wd[...])
        gate_grad = (hidden_grad * coef_g[at, :]).astype(BF16)
        up_grad = (hidden_grad * coef_u[at, :]).astype(BF16)
        con_t[at, :] = (dot_nt(gate_grad, wg[...]) + dot_nt(up_grad, wu[...])).astype(BF16)
        return carry

    sums = ((con_m, pair_m, row_m, col_m, mixed_ref), (con_t, pair_t, row_t, col_t, tgrad_ref))

    def pair(t):
        con, pairs = sums[t][:2]
        return pltpu.make_async_remote_copy(
            src_ref=con.at[half : 2 * half, :],
            dst_ref=pairs,
            send_sem=pair_send.at[t],
            recv_sem=pair_recv.at[t],
            device_id={"expert": other},
            device_id_type=MESH,
        )

    def line_at(rq):
        return pl.ds(pl.multiple_of(lax.rem(q + rq, SIDE) * (SIDE * rows), SIDE * rows), SIDE * rows)

    def to_line(t, r):
        con, _, lines = sums[t][:3]
        return pltpu.make_async_remote_copy(
            src_ref=con.at[line_at(r), :],
            dst_ref=lines.at[r - 1],
            send_sem=row_send.at[t, r - 1],
            recv_sem=row_recv.at[t, r - 1],
            device_id={"expert": peer(0, r)},
            device_id_type=MESH,
        )

    def send_lines(t):
        con, pairs = sums[t][:2]
        pair(t).wait_recv()
        for r in (2, 1, 3):
            at = line_at(r)
            con[at, :] = (con[at, :].astype(F32) + pairs[at, :].astype(F32)).astype(BF16)
            to_line(t, r).start()

    def block_at(r):
        return pl.multiple_of(lax.rem(q, SIDE) * (SIDE * rows) + lax.rem(p + r, SIDE) * rows, rows)

    def to_block(t, r):
        con, columns = sums[t][0], sums[t][3]
        return pltpu.make_async_remote_copy(
            src_ref=con.at[pl.ds(block_at(r), rows), :],
            dst_ref=columns.at[r - 1],
            send_sem=col_send.at[t, r - 1],
            recv_sem=col_recv.at[t, r - 1],
            device_id={"expert": peer(r, 0)},
            device_id_type=MESH,
        )

    def line_sum(t, r):
        con, pairs, lines = sums[t][:3]
        at = pl.ds(block_at(r), rows)
        inner = pl.ds(pl.multiple_of(lax.rem(p + r, SIDE) * rows, rows), rows)
        total = con[at, :].astype(F32) + pairs[at, :].astype(F32)
        for k in range(SIDE - 1):
            total = total + lines[k, inner, :].astype(F32)
        return total

    def send_blocks(t):
        con = sums[t][0]
        for r in range(1, SIDE):
            to_line(t, r).wait_recv()
        for r in (2, 1, 3):
            con[pl.ds(block_at(r), rows), :] = line_sum(t, r).astype(BF16)
            to_block(t, r).start()

    def finish(t):
        columns, out = sums[t][3:]
        total = line_sum(t, 0)
        for r in range(1, SIDE):
            to_block(t, r).wait_recv()
            total = total + columns[r - 1].astype(F32)
        out[...] = total.astype(BF16)

    for load in loads[4:]:
        load.wait()
    lax.fori_loop(tiles, 2 * tiles, outputs, 0)
    pair(0).start()
    lax.fori_loop(0, tiles, outputs, 0)
    relay(14, -14, 12, -12)
    relay(9, -9, 7, -7, 4, -4, 2, -2)
    lax.fori_loop(tiles, 2 * tiles, backward, 0)
    pair(1).start()
    relay(13, -13)
    send_lines(0)
    lax.fori_loop(0, tiles, backward, 0)
    relay(8, -8)
    send_lines(1)
    send_blocks(0)
    relay(3, -3)
    send_blocks(1)
    finish(0)
    finish(1)
    total = add_up(0)
    for i in range(2):
        down_ref[i] = total[:, i * hid : (i + 1) * hid]

    for t in range(2):
        for rp in range(SIDE):
            for rq in range(SIDE):
                cross(t, rp, rq).wait_send()
                if rp or rq:
                    gather(t, rp, rq).wait_send()
        pair(t).wait_send()
        for r in range(1, SIDE):
            to_line(t, r).wait_send()
            to_block(t, r).wait_send()
    for far in NEXT:
        travel(far).wait_send()


def on_device(n_dp, experts, tokens, expert_ids, gate_probs, w_gate, w_up, w_down, out_grad):
    rows, width = tokens.shape
    mine, _, hid = w_gate.shape
    half = CHIPS * rows
    share = width // n_dp
    vmem = pl.BlockSpec(memory_space=pltpu.VMEM)
    hbm = pl.BlockSpec(memory_space=pl.ANY)
    dma = pltpu.SemaphoreType.DMA
    reach = SIDE - 1
    mixed, token_grad, down = pl.pallas_call(
        lambda *refs: layer_kernel(n_dp, *refs),
        out_shape=(
            jax.ShapeDtypeStruct((rows, width), BF16),
            jax.ShapeDtypeStruct((rows, width), BF16),
            jax.ShapeDtypeStruct((mine, share, hid), F32),
        ),
        in_specs=[hbm] * 7,
        out_specs=(vmem, vmem, vmem),
        scratch_shapes=[
            pltpu.VMEM(expert_ids.shape[::-1], jnp.int32),
            pltpu.VMEM(gate_probs.shape[::-1], F32),
            pltpu.VMEM((2 * half, width + 2 * experts), BF16),
            pltpu.VMEM((2 * half, width), BF16),
            pltpu.VMEM((width, mine * hid), BF16),
            pltpu.VMEM((width, mine * hid), BF16),
            pltpu.VMEM((mine * hid, width), BF16),
            pltpu.VMEM((2 * half, mine * hid), F32),
            pltpu.VMEM((2 * half, mine * hid), F32),
            pltpu.VMEM((2 * half, mine * hid), BF16),
            pltpu.VMEM((2 * half, width), BF16),
            pltpu.VMEM((2 * half, width), BF16),
            pltpu.VMEM((half, width), BF16),
            pltpu.VMEM((half, width), BF16),
            pltpu.VMEM((reach, SIDE * rows, width), BF16),
            pltpu.VMEM((reach, SIDE * rows, width), BF16),
            pltpu.VMEM((reach, rows, width), BF16),
            pltpu.VMEM((reach, rows, width), BF16),
            pltpu.VMEM((width, mine * hid), BF16),
            pltpu.VMEM((len(NEXT), share, mine * hid), BF16),
            dma((4,)),
            dma((3, 2)),
            dma((2, SIDE, SIDE)),
            dma((2, SIDE, SIDE)),
            dma((2, SIDE, SIDE)),
            dma((2, SIDE, SIDE)),
            dma((2,)),
            dma((2,)),
            dma((2, reach)),
            dma((2, reach)),
            dma((2, reach)),
            dma((2, reach)),
            dma((len(NEXT),)),
            dma((len(NEXT),)),
        ],
        compiler_params=pltpu.CompilerParams(
            collective_id=0, has_side_effects=True, vmem_limit_bytes=58 * 1024 * 1024
        ),
    )(tokens, expert_ids.T, gate_probs.T, w_gate, w_up, w_down, out_grad)
    return mixed, token_grad, jnp.transpose(down, (0, 2, 1))


def solution(mesh):
    n_dp = mesh.shape["dp"]

    def body(*args):
        return on_device(n_dp, args[3].shape[0] * mesh.shape["expert"], *args)

    return jax.shard_map(
        body,
        mesh=mesh,
        in_specs=(
            P(("expert", "dp"), None),
            P(("expert", "dp"), None),
            P(("expert", "dp"), None),
            P("expert", None, None),
            P("expert", None, None),
            P("expert", None, None),
            P(("expert", "dp"), None),
        ),
        out_specs=(P(("expert", "dp"), None), P(("expert", "dp"), None), P("expert", None, "dp")),
        check_vma=False,
    )
```

```python
import jax
import jax.numpy as jnp
from jax import lax
from jax.experimental import pallas as pl
from jax.experimental.pallas import tpu as pltpu
from jax.sharding import PartitionSpec as P

MESH = pl.DeviceIdType.MESH
F32 = jnp.float32
BF16 = jnp.bfloat16
SIDE = 4
CHIPS = SIDE * SIDE
TILE = 256
CAP = 8

PARENT = {1: 2, 2: 3, 3: 0, 4: 3, 5: 4, 6: 7, 7: 8, 8: 3, 9: 8, 10: 9, 11: 12, 12: 13, 13: 8, 14: 13, 15: 14, 16: 14}
NEXT = dict(PARENT)
NEXT.update({-far: -near for far, near in PARENT.items() if far < 16})
FROM = {near: [far for far in NEXT if NEXT[far] == near] for near in set(NEXT.values())}


def dot(a, b):
    return lax.dot_general(a, b, (((1,), (0,)), ((), ())), preferred_element_type=F32)


def dot_nt(a, b):
    return lax.dot_general(a, b, (((1,), (1,)), ((), ())), preferred_element_type=F32)


def dot_tn(a, b):
    return lax.dot_general(a, b, (((0,), (0,)), ((), ())), preferred_element_type=F32)


def layer_kernel(
    n_dp,
    tok_hbm, ids_hbm, prob_hbm, wg_hbm, wu_hbm, wd_hbm, grad_hbm,
    mixed_ref, tgrad_ref, down_ref,
    ids_ref, prob_ref, x_all, dy_all, wg, wu, wd, slots, xs, dys, coef_g, coef_u, ph, outs, back, con_m, con_t, pair_m, pair_t, row_m, row_t, col_m, col_t, part, ring,
    own_sem, w_sem, ag_send, ag_recv, in_send, in_recv, pair_send, pair_recv, row_send, row_recv, col_send, col_recv, z_send, z_recv,
):
    e = lax.axis_index("expert")
    z = lax.axis_index("dp")
    rows, width = tok_hbm.shape
    half = CHIPS * rows
    hid = wg_hbm.shape[2]
    share = width // n_dp
    c = lax.rem(e, 2)
    x = lax.rem(lax.div(e, 2), SIDE)
    y = lax.div(e, 2 * SIDE)
    p = x + c * (y - x)
    q = y + c * (x - y)
    other = e + 1 - 2 * c

    def peer(dp, dq):
        p2, q2 = lax.rem(p + dp, SIDE), lax.rem(q + dq, SIDE)
        x2, y2 = p2 + c * (q2 - p2), q2 + c * (p2 - q2)
        return (y2 * SIDE + x2) * 2 + c

    def block(rp, rq):
        slot = lax.rem(q + SIDE - rq, SIDE) * SIDE + lax.rem(p + SIDE - rp, SIDE)
        return pl.multiple_of(slot * rows, rows)

    mine = block(0, 0)
    own = [
        pltpu.make_async_copy(ids_hbm, ids_ref, own_sem.at[0]),
        pltpu.make_async_copy(prob_hbm, prob_ref, own_sem.at[1]),
        pltpu.make_async_copy(tok_hbm, x_all.at[pl.ds(mine, rows), :width], own_sem.at[2]),
        pltpu.make_async_copy(grad_hbm, dy_all.at[pl.ds(mine, rows), :], own_sem.at[3]),
    ]
    for load in own:
        load.start()

    loads = []
    for k, (src, dst) in enumerate(((wg_hbm, wg), (wu_hbm, wu), (wd_hbm, wd))):
        load = pltpu.make_async_copy(src, dst, w_sem.at[k])
        load.start()
        loads.append(load)

    barrier = pltpu.get_barrier_semaphore()
    near = [{"expert": other}]
    for r in range(1, SIDE):
        near.append({"expert": peer(r, 0)})
        near.append({"expert": peer(0, r)})
    reach = sorted({NEXT[far] - far for far in NEXT})
    for r in reach:
        near.append({"dp": lax.rem(z + n_dp - r, n_dp)})
    for device in near:
        pl.semaphore_signal(barrier, inc=1, device_id=device, device_id_type=MESH)

    lanes = 128
    experts = 64
    gate_at, code_at = width, width + lanes
    expert_of = lax.broadcasted_iota(jnp.int32, (experts, rows), 0)
    own[0].wait()
    own[1].wait()
    gates = jnp.zeros((experts, rows), F32)
    taken = jnp.zeros((experts, rows), F32)
    for k in range(ids_ref.shape[0]):
        hit = ids_ref[k : k + 1, :] == expert_of
        gates = gates + jnp.where(hit, prob_ref[k : k + 1, :], 0.0)
        taken = taken + jnp.where(hit, 1.0, 0.0)
    high = gates.astype(BF16)
    low = (gates - high.astype(F32)).astype(BF16)
    before = lax.broadcasted_iota(jnp.int32, (rows, rows), 0) < lax.broadcasted_iota(jnp.int32, (rows, rows), 1)
    rank = dot(taken.astype(BF16), before.astype(F32).astype(BF16))
    code = (taken * (rank + 1.0) - 1.0).astype(BF16)
    line = lax.broadcasted_iota(jnp.int32, (experts, lanes), 0)
    lane = lax.broadcasted_iota(jnp.int32, (experts, lanes), 1)
    first = (line == lane).astype(F32).astype(BF16)
    second = (line + experts == lane).astype(F32).astype(BF16)
    x_all[pl.ds(mine, rows), gate_at:code_at] = (dot_tn(high, first) + dot_tn(low, second)).astype(BF16)
    x_all[pl.ds(mine, rows), code_at:] = dot_tn(code, first).astype(BF16)
    own[2].wait()
    own[3].wait()

    arrays = (x_all, dy_all)

    def gather(t, rp, rq):
        at = block(0, 0) if rq == 0 else block(rp, 0)
        ref = arrays[t].at[pl.ds(at, rows), :]
        return pltpu.make_async_remote_copy(
            src_ref=ref,
            dst_ref=ref,
            send_sem=ag_send.at[t, rp, rq],
            recv_sem=ag_recv.at[t, rp, rq],
            device_id={"expert": peer(rp, 0) if rq == 0 else peer(0, rq)},
            device_id_type=MESH,
        )

    def cross(t, rp, rq):
        at = block(rp, rq)
        return pltpu.make_async_remote_copy(
            src_ref=arrays[t].at[pl.ds(at, rows), :],
            dst_ref=arrays[t].at[pl.ds(pl.multiple_of(half + at, rows), rows), :],
            send_sem=in_send.at[t, rp, rq],
            recv_sem=in_recv.at[t, rp, rq],
            device_id={"expert": other},
            device_id_type=MESH,
        )

    pl.semaphore_wait(barrier, len(near))

    for t in range(2):
        for r in range(1, SIDE):
            gather(t, r, 0).start()
        for r in range(1, SIDE):
            gather(t, 0, r).start()
        cross(t, 0, 0).start()
    for t in range(2):
        for rp in (1, 3, 2):
            gather(t, rp, 0).wait_recv()
            for rq in range(1, SIDE):
                gather(t, rp, rq).start()
            cross(t, rp, 0).start()

    def pass_on(t):
        for rp in range(SIDE):
            for rq in range(1, SIDE):
                gather(t, rp, rq).wait_recv()
                cross(t, rp, rq).start()

    per = TILE // rows * CAP
    line = lax.broadcasted_iota(jnp.int32, (lanes, 2 * per), 0)
    lane = lax.broadcasted_iota(jnp.int32, (lanes, 2 * per), 1)
    pick_code = (line == jnp.where(lane >= per, 2 * e + 1, 2 * e)).astype(F32).astype(BF16)
    token = lax.broadcasted_iota(jnp.int32, (TILE, 2 * per), 0)
    place = lax.broadcasted_iota(jnp.int32, (TILE, 2 * per), 1)
    place = jnp.where(place >= per, place - per, place)
    same = jnp.where((token >> 5) == (place >> 3), 1.0, 0.0)
    wanted = (place & (CAP - 1)).astype(F32)

    def tile_at(i):
        return pl.ds(pl.multiple_of(i * TILE, TILE), TILE)

    def rows_at(i):
        return pl.ds(pl.multiple_of(i * per, per), per)

    def pack_x(i, carry):
        at = tile_at(i)
        codes = dot(x_all[at, code_at:], pick_code)
        chosen = (jnp.where(codes == wanted, 1.0, 0.0) * same).astype(BF16)
        slots[at, :] = chosen
        got = dot_tn(chosen, x_all[at, :code_at]).astype(BF16)
        xs[0, rows_at(i), :] = got[:per]
        xs[1, rows_at(i), :] = got[per:]
        return carry

    def pack_dy(i, carry):
        got = dot_tn(slots[tile_at(i), :], dy_all[tile_at(i), :]).astype(BF16)
        dys[0, rows_at(i), :] = got[:per]
        dys[1, rows_at(i), :] = got[per:]
        return carry

    gate_line = lax.broadcasted_iota(jnp.int32, (lanes, hid), 0)
    gate_line = jnp.where(gate_line >= experts, gate_line - experts, gate_line)

    def forward(k, carry):
        gate = dot(xs[k, :, :width], wg[k])
        up = dot(xs[k, :, :width], wu[k])
        prob = dot(xs[k, :, gate_at:], (gate_line == 2 * e + k).astype(F32).astype(BF16))
        sig = jax.nn.sigmoid(gate)
        scaled = prob * (gate * sig)
        ph[k] = (scaled * up).astype(BF16)
        coef_u[k] = scaled
        coef_g[k] = prob * up * sig * (1.0 + gate * (1.0 - sig))
        return carry

    tiles = half // TILE
    pass_on(0)
    lax.fori_loop(0, tiles, pack_x, 0)
    for rp in range(SIDE):
        for rq in range(SIDE):
            cross(0, rp, rq).wait_recv()
    lax.fori_loop(tiles, 2 * tiles, pack_x, 0)
    pass_on(1)
    for load in loads:
        load.wait()
    lax.fori_loop(0, 2, forward, 0)
    lax.fori_loop(0, tiles, pack_dy, 0)
    for rp in range(SIDE):
        for rq in range(SIDE):
            cross(1, rp, rq).wait_recv()
    lax.fori_loop(tiles, 2 * tiles, pack_dy, 0)

    def partial(i, carry):
        at = tile_at(i)
        for k in range(2):
            part[at, k * hid : (k + 1) * hid] = dot_tn(dys[k, :, at], ph[k]).astype(BF16)
        return carry

    lax.fori_loop(0, width // TILE, partial, 0)

    def owned(far):
        owner = lax.rem(z + n_dp - far, n_dp)
        return pl.ds(pl.multiple_of(owner * share, share), share)

    def travel(far):
        src = ring.at[slot_of[FROM[far][0]]] if far in FROM else part.at[owned(far), :]
        return pltpu.make_async_remote_copy(
            src_ref=src,
            dst_ref=ring.at[slot_of[far]],
            send_sem=z_send.at[slot_of[far]],
            recv_sem=z_recv.at[slot_of[far]],
            device_id={"dp": lax.rem(z + n_dp + NEXT[far] - far, n_dp)},
            device_id_type=MESH,
        )

    slot_of = {far: k for k, far in enumerate(sorted(NEXT))}

    def add_up(far):
        total = part[owned(far), :].astype(F32)
        for child in FROM[far]:
            travel(child).wait_recv()
            total = total + ring[slot_of[child]].astype(F32)
        return total

    def relay(*fars):
        for far in fars:
            ring[slot_of[FROM[far][0]]] = add_up(far).astype(BF16)
            travel(far).start()

    def begin(*fars):
        for far in fars:
            travel(far).start()

    begin(16, 15, -15, 11, -11)

    def outputs(k, carry):
        outs[k] = dot(ph[k], wd[k]).astype(BF16)
        return carry

    def backward(k, carry):
        hidden_grad = dot_nt(dys[k], wd[k])
        gate_grad = (hidden_grad * coef_g[k]).astype(BF16)
        up_grad = (hidden_grad * coef_u[k]).astype(BF16)
        back[k] = (dot_nt(gate_grad, wg[k]) + dot_nt(up_grad, wu[k])).astype(BF16)
        return carry

    def unpack(source, con):
        def one(i, carry):
            both = jnp.concatenate([source[0, rows_at(i), :], source[1, rows_at(i), :]], axis=0)
            con[tile_at(i), :] = dot(slots[tile_at(i), :], both).astype(BF16)
            return carry

        return one

    sums = ((con_m, pair_m, row_m, col_m, mixed_ref), (con_t, pair_t, row_t, col_t, tgrad_ref))

    def pair(t, r):
        con, pairs = sums[t][:2]
        at = lax.rem(p + r, SIDE) * (SIDE * rows)
        return pltpu.make_async_remote_copy(
            src_ref=con.at[pl.ds(pl.multiple_of(half + at, SIDE * rows), SIDE * rows), :],
            dst_ref=pairs.at[pl.ds(pl.multiple_of(at, SIDE * rows), SIDE * rows), :],
            send_sem=pair_send.at[t, r],
            recv_sem=pair_recv.at[t, r],
            device_id={"expert": other},
            device_id_type=MESH,
        )

    def send_pairs(t):
        for r in (2, 1, 3, 0):
            pair(t, r).start()

    def line_at(rq):
        return pl.ds(pl.multiple_of(lax.rem(q + rq, SIDE) * (SIDE * rows), SIDE * rows), SIDE * rows)

    def to_line(t, r):
        con, _, lines = sums[t][:3]
        return pltpu.make_async_remote_copy(
            src_ref=con.at[line_at(r), :],
            dst_ref=lines.at[r - 1],
            send_sem=row_send.at[t, r - 1],
            recv_sem=row_recv.at[t, r - 1],
            device_id={"expert": peer(0, r)},
            device_id_type=MESH,
        )

    def send_lines(t):
        con, pairs = sums[t][:2]
        for r in (2, 1, 3):
            at = line_at(r)
            pair(t, r).wait_recv()
            con[at, :] = (con[at, :].astype(F32) + pairs[at, :].astype(F32)).astype(BF16)
            to_line(t, r).start()

    def block_at(r):
        return pl.multiple_of(lax.rem(q, SIDE) * (SIDE * rows) + lax.rem(p + r, SIDE) * rows, rows)

    def to_block(t, r):
        con, columns = sums[t][0], sums[t][3]
        return pltpu.make_async_remote_copy(
            src_ref=con.at[pl.ds(block_at(r), rows), :],
            dst_ref=columns.at[r - 1],
            send_sem=col_send.at[t, r - 1],
            recv_sem=col_recv.at[t, r - 1],
            device_id={"expert": peer(r, 0)},
            device_id_type=MESH,
        )

    def line_sum(t, r):
        con, pairs, lines = sums[t][:3]
        at = pl.ds(block_at(r), rows)
        inner = pl.ds(pl.multiple_of(lax.rem(p + r, SIDE) * rows, rows), rows)
        total = con[at, :].astype(F32) + pairs[at, :].astype(F32)
        for k in range(SIDE - 1):
            total = total + lines[k, inner, :].astype(F32)
        return total

    def send_blocks(t):
        con = sums[t][0]
        pair(t, 0).wait_recv()
        for r in range(1, SIDE):
            to_line(t, r).wait_recv()
        for r in (2, 1, 3):
            con[pl.ds(block_at(r), rows), :] = line_sum(t, r).astype(BF16)
            to_block(t, r).start()

    def finish(t):
        columns, out = sums[t][3:]
        total = line_sum(t, 0)
        for r in range(1, SIDE):
            to_block(t, r).wait_recv()
            total = total + columns[r - 1].astype(F32)
        out[...] = total.astype(BF16)

    lax.fori_loop(0, 2, outputs, 0)
    lax.fori_loop(tiles, 2 * tiles, unpack(outs, con_m), 0)
    send_pairs(0)
    begin(10, -10, 6, -6)
    lax.fori_loop(0, 2, backward, 0)
    lax.fori_loop(tiles, 2 * tiles, unpack(back, con_t), 0)
    send_pairs(1)
    relay(14, -14, 12, -12)
    begin(5, -5, 1, -1)
    lax.fori_loop(0, tiles, unpack(outs, con_m), 0)
    send_lines(0)
    lax.fori_loop(0, tiles, unpack(back, con_t), 0)
    relay(13, -13)
    relay(9, -9, 7, -7)
    send_lines(1)
    relay(4, -4, 2, -2)
    send_blocks(0)
    relay(8, -8)
    send_blocks(1)
    finish(0)
    relay(3, -3)
    finish(1)
    total = add_up(0)
    for i in range(2):
        down_ref[i] = total[:, i * hid : (i + 1) * hid]

    for t in range(2):
        for rp in range(SIDE):
            for rq in range(SIDE):
                cross(t, rp, rq).wait_send()
                if rp or rq:
                    gather(t, rp, rq).wait_send()
        for r in range(SIDE):
            pair(t, r).wait_send()
        for r in range(1, SIDE):
            to_line(t, r).wait_send()
            to_block(t, r).wait_send()
    for far in NEXT:
        travel(far).wait_send()


def on_device(n_dp, tokens, expert_ids, gate_probs, w_gate, w_up, w_down, out_grad):
    rows, width = tokens.shape
    mine, _, hid = w_gate.shape
    half = CHIPS * rows
    share = width // n_dp
    taken = 2 * CHIPS * CAP
    vmem = pl.BlockSpec(memory_space=pltpu.VMEM)
    hbm = pl.BlockSpec(memory_space=pltpu.HBM)
    dma = pltpu.SemaphoreType.DMA
    reach = SIDE - 1
    mixed, token_grad, down = pl.pallas_call(
        lambda *refs: layer_kernel(n_dp, *refs),
        out_shape=(
            jax.ShapeDtypeStruct((rows, width), BF16),
            jax.ShapeDtypeStruct((rows, width), BF16),
            jax.ShapeDtypeStruct((mine, share, hid), F32),
        ),
        in_specs=[hbm] * 7,
        out_specs=(vmem, vmem, vmem),
        scratch_shapes=[
            pltpu.VMEM(expert_ids.shape[::-1], jnp.int32),
            pltpu.VMEM(gate_probs.shape[::-1], F32),
            pltpu.VMEM((2 * half, width + 256), BF16),
            pltpu.VMEM((2 * half, width), BF16),
            pltpu.VMEM((mine, width, hid), BF16),
            pltpu.VMEM((mine, width, hid), BF16),
            pltpu.VMEM((mine, hid, width), BF16),
            pltpu.VMEM((2 * half, 2 * TILE // rows * CAP), BF16),
            pltpu.VMEM((mine, taken, width + 128), BF16),
            pltpu.VMEM((mine, taken, width), BF16),
            pltpu.VMEM((mine, taken, hid), F32),
            pltpu.VMEM((mine, taken, hid), F32),
            pltpu.VMEM((mine, taken, hid), BF16),
            pltpu.VMEM((mine, taken, width), BF16),
            pltpu.VMEM((mine, taken, width), BF16),
            pltpu.VMEM((2 * half, width), BF16),
            pltpu.VMEM((2 * half, width), BF16),
            pltpu.VMEM((half, width), BF16),
            pltpu.VMEM((half, width), BF16),
            pltpu.VMEM((reach, SIDE * rows, width), BF16),
            pltpu.VMEM((reach, SIDE * rows, width), BF16),
            pltpu.VMEM((reach, rows, width), BF16),
            pltpu.VMEM((reach, rows, width), BF16),
            pltpu.VMEM((width, mine * hid), BF16),
            pltpu.VMEM((len(NEXT), share, mine * hid), BF16),
            dma((4,)),
            dma((3,)),
            dma((2, SIDE, SIDE)),
            dma((2, SIDE, SIDE)),
            dma((2, SIDE, SIDE)),
            dma((2, SIDE, SIDE)),
            dma((2, SIDE)),
            dma((2, SIDE)),
            dma((2, reach)),
            dma((2, reach)),
            dma((2, reach)),
            dma((2, reach)),
            dma((len(NEXT),)),
            dma((len(NEXT),)),
        ],
        compiler_params=pltpu.CompilerParams(
            collective_id=0, has_side_effects=True, vmem_limit_bytes=58 * 1024 * 1024
        ),
    )(tokens, expert_ids.T, gate_probs.T, w_gate, w_up, w_down, out_grad)
    return mixed, token_grad, jnp.transpose(down, (0, 2, 1))


def solution(mesh):
    n_dp = mesh.shape["dp"]

    def body(*args):
        return on_device(n_dp, *args)

    return jax.shard_map(
        body,
        mesh=mesh,
        in_specs=(
            P(("expert", "dp"), None),
            P(("expert", "dp"), None),
            P(("expert", "dp"), None),
            P("expert", None, None),
            P("expert", None, None),
            P("expert", None, None),
            P(("expert", "dp"), None),
        ),
        out_specs=(P(("expert", "dp"), None), P(("expert", "dp"), None), P("expert", None, "dp")),
        check_vma=False,
    )
```

```python
import jax
import jax.numpy as jnp
from jax import lax
from jax.experimental import pallas as pl
from jax.experimental.pallas import tpu as pltpu
from jax.sharding import PartitionSpec as P

MESH = pl.DeviceIdType.MESH
F32 = jnp.float32
BF16 = jnp.bfloat16
SIDE = 4
CHIPS = SIDE * SIDE
TILE = 256
CAP = 8

PARENT = {1: 2, 2: 3, 3: 0, 4: 3, 5: 4, 6: 7, 7: 8, 8: 3, 9: 8, 10: 9, 11: 12, 12: 13, 13: 8, 14: 13, 15: 14, 16: 14}
NEXT = dict(PARENT)
NEXT.update({-far: -near for far, near in PARENT.items() if far < 16})
FROM = {near: [far for far in NEXT if NEXT[far] == near] for near in set(NEXT.values())}


def dot(a, b):
    return lax.dot_general(a, b, (((1,), (0,)), ((), ())), preferred_element_type=F32)


def dot_nt(a, b):
    return lax.dot_general(a, b, (((1,), (1,)), ((), ())), preferred_element_type=F32)


def dot_tn(a, b):
    return lax.dot_general(a, b, (((0,), (0,)), ((), ())), preferred_element_type=F32)


def layer_kernel(
    n_dp,
    tok_hbm, ids_hbm, prob_hbm, wg_hbm, wu_hbm, wd_hbm, grad_hbm,
    mixed_ref, tgrad_ref, down_ref,
    ids_ref, prob_ref, x_all, dy_all, wg, wu, wd, slots, xs, dys, coef_g, coef_u, ph, outs, back, con_m, con_t, pair_m, pair_t, row_m, row_t, col_m, col_t, part, ring,
    own_sem, w_sem, ag_send, ag_recv, in_send, in_recv, pair_send, pair_recv, row_send, row_recv, col_send, col_recv, z_send, z_recv,
):
    e = lax.axis_index("expert")
    z = lax.axis_index("dp")
    rows, width = tok_hbm.shape
    half = CHIPS * rows
    hid = wg_hbm.shape[2]
    share = width // n_dp
    c = lax.rem(e, 2)
    x = lax.rem(lax.div(e, 2), SIDE)
    y = lax.div(e, 2 * SIDE)
    p = x + c * (y - x)
    q = y + c * (x - y)
    other = e + 1 - 2 * c

    def peer(dp, dq):
        p2, q2 = lax.rem(p + dp, SIDE), lax.rem(q + dq, SIDE)
        x2, y2 = p2 + c * (q2 - p2), q2 + c * (p2 - q2)
        return (y2 * SIDE + x2) * 2 + c

    def block(rp, rq):
        slot = lax.rem(q + SIDE - rq, SIDE) * SIDE + lax.rem(p + SIDE - rp, SIDE)
        return pl.multiple_of(slot * rows, rows)

    mine = block(0, 0)
    own = [
        pltpu.make_async_copy(ids_hbm, ids_ref, own_sem.at[0]),
        pltpu.make_async_copy(prob_hbm, prob_ref, own_sem.at[1]),
        pltpu.make_async_copy(tok_hbm, x_all.at[pl.ds(mine, rows), :width], own_sem.at[2]),
        pltpu.make_async_copy(grad_hbm, dy_all.at[pl.ds(mine, rows), :], own_sem.at[3]),
    ]
    for load in own:
        load.start()

    loads = []
    for k, (src, dst) in enumerate(((wg_hbm, wg), (wu_hbm, wu), (wd_hbm, wd))):
        load = pltpu.make_async_copy(src, dst, w_sem.at[k])
        load.start()
        loads.append(load)

    barrier = pltpu.get_barrier_semaphore()
    near = [{"expert": other}]
    for r in range(1, SIDE):
        near.append({"expert": peer(r, 0)})
        near.append({"expert": peer(0, r)})
    reach = sorted({NEXT[far] - far for far in NEXT})
    for r in reach:
        near.append({"dp": lax.rem(z + n_dp - r, n_dp)})
    for device in near:
        pl.semaphore_signal(barrier, inc=1, device_id=device, device_id_type=MESH)

    lanes = 128
    experts = 64
    gate_at, code_at = width, width + lanes
    expert_of = lax.broadcasted_iota(jnp.int32, (experts, rows), 0)
    own[0].wait()
    own[1].wait()
    gates = jnp.zeros((experts, rows), F32)
    taken = jnp.zeros((experts, rows), F32)
    for k in range(ids_ref.shape[0]):
        hit = ids_ref[k : k + 1, :] == expert_of
        gates = gates + jnp.where(hit, prob_ref[k : k + 1, :], 0.0)
        taken = taken + jnp.where(hit, 1.0, 0.0)
    high = gates.astype(BF16)
    low = (gates - high.astype(F32)).astype(BF16)
    before = lax.broadcasted_iota(jnp.int32, (rows, rows), 0) < lax.broadcasted_iota(jnp.int32, (rows, rows), 1)
    rank = dot(taken.astype(BF16), before.astype(F32).astype(BF16))
    code = (taken * (rank + 1.0) - 1.0).astype(BF16)
    line = lax.broadcasted_iota(jnp.int32, (experts, lanes), 0)
    lane = lax.broadcasted_iota(jnp.int32, (experts, lanes), 1)
    first = (line == lane).astype(F32).astype(BF16)
    second = (line + experts == lane).astype(F32).astype(BF16)
    x_all[pl.ds(mine, rows), gate_at:code_at] = (dot_tn(high, first) + dot_tn(low, second)).astype(BF16)
    x_all[pl.ds(mine, rows), code_at:] = dot_tn(code, first).astype(BF16)
    own[2].wait()
    own[3].wait()

    arrays = (x_all, dy_all)

    def gather(t, rp, rq):
        at = block(0, 0) if rq == 0 else block(rp, 0)
        ref = arrays[t].at[pl.ds(at, rows), :]
        return pltpu.make_async_remote_copy(
            src_ref=ref,
            dst_ref=ref,
            send_sem=ag_send.at[t, rp, rq],
            recv_sem=ag_recv.at[t, rp, rq],
            device_id={"expert": peer(rp, 0) if rq == 0 else peer(0, rq)},
            device_id_type=MESH,
        )

    def cross(t, rp, rq):
        at = block(rp, rq)
        return pltpu.make_async_remote_copy(
            src_ref=arrays[t].at[pl.ds(at, rows), :],
            dst_ref=arrays[t].at[pl.ds(pl.multiple_of(half + at, rows), rows), :],
            send_sem=in_send.at[t, rp, rq],
            recv_sem=in_recv.at[t, rp, rq],
            device_id={"expert": other},
            device_id_type=MESH,
        )

    pl.semaphore_wait(barrier, len(near))

    for t in range(2):
        for r in range(1, SIDE):
            gather(t, r, 0).start()
        for r in range(1, SIDE):
            gather(t, 0, r).start()
        cross(t, 0, 0).start()
    for t in range(2):
        for rp in (1, 3, 2):
            gather(t, rp, 0).wait_recv()
            for rq in range(1, SIDE):
                gather(t, rp, rq).start()
            cross(t, rp, 0).start()

    def pass_on(t):
        for rp in range(SIDE):
            for rq in range(1, SIDE):
                gather(t, rp, rq).wait_recv()
                cross(t, rp, rq).start()

    per = TILE // rows * CAP
    line = lax.broadcasted_iota(jnp.int32, (lanes, 2 * per), 0)
    lane = lax.broadcasted_iota(jnp.int32, (lanes, 2 * per), 1)
    pick_code = (line == jnp.where(lane >= per, 2 * e + 1, 2 * e)).astype(F32).astype(BF16)
    token = lax.broadcasted_iota(jnp.int32, (TILE, 2 * per), 0)
    place = lax.broadcasted_iota(jnp.int32, (TILE, 2 * per), 1)
    place = jnp.where(place >= per, place - per, place)
    same = jnp.where((token >> 5) == (place >> 3), 1.0, 0.0)
    wanted = (place & (CAP - 1)).astype(F32)

    def tile_at(i):
        return pl.ds(pl.multiple_of(i * TILE, TILE), TILE)

    def rows_at(i):
        return pl.ds(pl.multiple_of(i * per, per), per)

    def pack_x(i, carry):
        at = tile_at(i)
        codes = dot(x_all[at, code_at:], pick_code)
        chosen = (jnp.where(codes == wanted, 1.0, 0.0) * same).astype(BF16)
        slots[at, :] = chosen
        got = dot_tn(chosen, x_all[at, :code_at]).astype(BF16)
        xs[0, rows_at(i), :] = got[:per]
        xs[1, rows_at(i), :] = got[per:]
        return carry

    def pack_dy(i, carry):
        got = dot_tn(slots[tile_at(i), :], dy_all[tile_at(i), :]).astype(BF16)
        dys[0, rows_at(i), :] = got[:per]
        dys[1, rows_at(i), :] = got[per:]
        return carry

    gate_line = lax.broadcasted_iota(jnp.int32, (lanes, hid), 0)
    gate_line = jnp.where(gate_line >= experts, gate_line - experts, gate_line)

    def forward(k, carry):
        gate = dot(xs[k, :, :width], wg[k])
        up = dot(xs[k, :, :width], wu[k])
        prob = dot(xs[k, :, gate_at:], (gate_line == 2 * e + k).astype(F32).astype(BF16))
        sig = jax.nn.sigmoid(gate)
        scaled = prob * (gate * sig)
        ph[k] = (scaled * up).astype(BF16)
        coef_u[k] = scaled
        coef_g[k] = prob * up * sig * (1.0 + gate * (1.0 - sig))
        return carry

    tiles = half // TILE
    pass_on(0)
    lax.fori_loop(0, tiles, pack_x, 0)
    for rp in range(SIDE):
        for rq in range(SIDE):
            cross(0, rp, rq).wait_recv()
    lax.fori_loop(tiles, 2 * tiles, pack_x, 0)
    pass_on(1)
    for load in loads:
        load.wait()
    lax.fori_loop(0, 2, forward, 0)
    lax.fori_loop(0, tiles, pack_dy, 0)
    for rp in range(SIDE):
        for rq in range(SIDE):
            cross(1, rp, rq).wait_recv()
    lax.fori_loop(tiles, 2 * tiles, pack_dy, 0)

    def partial(i, carry):
        at = tile_at(i)
        for k in range(2):
            part[at, k * hid : (k + 1) * hid] = dot_tn(dys[k, :, at], ph[k]).astype(BF16)
        return carry

    lax.fori_loop(0, width // TILE, partial, 0)

    def owned(far):
        owner = lax.rem(z + n_dp - far, n_dp)
        return pl.ds(pl.multiple_of(owner * share, share), share)

    def travel(far):
        src = ring.at[slot_of[FROM[far][0]]] if far in FROM else part.at[owned(far), :]
        return pltpu.make_async_remote_copy(
            src_ref=src,
            dst_ref=ring.at[slot_of[far]],
            send_sem=z_send.at[slot_of[far]],
            recv_sem=z_recv.at[slot_of[far]],
            device_id={"dp": lax.rem(z + n_dp + NEXT[far] - far, n_dp)},
            device_id_type=MESH,
        )

    slot_of = {far: k for k, far in enumerate(sorted(NEXT))}

    def add_up(far):
        total = part[owned(far), :].astype(F32)
        for child in FROM[far]:
            travel(child).wait_recv()
            total = total + ring[slot_of[child]].astype(F32)
        return total

    def relay(*fars):
        for far in fars:
            ring[slot_of[FROM[far][0]]] = add_up(far).astype(BF16)
            travel(far).start()

    def begin(*fars):
        for far in fars:
            travel(far).start()

    begin(16, 15, -15, 11, -11)

    def outputs(k, carry):
        outs[k] = dot(ph[k], wd[k]).astype(BF16)
        return carry

    def backward(k, carry):
        hidden_grad = dot_nt(dys[k], wd[k])
        gate_grad = (hidden_grad * coef_g[k]).astype(BF16)
        up_grad = (hidden_grad * coef_u[k]).astype(BF16)
        back[k] = (dot_nt(gate_grad, wg[k]) + dot_nt(up_grad, wu[k])).astype(BF16)
        return carry

    def unpack(source, con):
        def one(i, carry):
            both = jnp.concatenate([source[0, rows_at(i), :], source[1, rows_at(i), :]], axis=0)
            con[tile_at(i), :] = dot(slots[tile_at(i), :], both).astype(BF16)
            return carry

        return one

    sums = ((con_m, pair_m, row_m, col_m, mixed_ref), (con_t, pair_t, row_t, col_t, tgrad_ref))

    def pair(t, r):
        con, pairs = sums[t][:2]
        at = lax.rem(p + r, SIDE) * (SIDE * rows)
        return pltpu.make_async_remote_copy(
            src_ref=con.at[pl.ds(pl.multiple_of(half + at, SIDE * rows), SIDE * rows), :],
            dst_ref=pairs.at[pl.ds(pl.multiple_of(at, SIDE * rows), SIDE * rows), :],
            send_sem=pair_send.at[t, r],
            recv_sem=pair_recv.at[t, r],
            device_id={"expert": other},
            device_id_type=MESH,
        )

    def send_pairs(t):
        for r in (2, 1, 3, 0):
            pair(t, r).start()

    def line_at(rq):
        return pl.ds(pl.multiple_of(lax.rem(q + rq, SIDE) * (SIDE * rows), SIDE * rows), SIDE * rows)

    def to_line(t, r):
        con, _, lines = sums[t][:3]
        return pltpu.make_async_remote_copy(
            src_ref=con.at[line_at(r), :],
            dst_ref=lines.at[r - 1],
            send_sem=row_send.at[t, r - 1],
            recv_sem=row_recv.at[t, r - 1],
            device_id={"expert": peer(0, r)},
            device_id_type=MESH,
        )

    def send_lines(t):
        con, pairs = sums[t][:2]
        for r in (2, 1, 3):
            at = line_at(r)
            pair(t, r).wait_recv()
            con[at, :] = (con[at, :].astype(F32) + pairs[at, :].astype(F32)).astype(BF16)
            to_line(t, r).start()

    def block_at(r):
        return pl.multiple_of(lax.rem(q, SIDE) * (SIDE * rows) + lax.rem(p + r, SIDE) * rows, rows)

    def to_block(t, r):
        con, columns = sums[t][0], sums[t][3]
        return pltpu.make_async_remote_copy(
            src_ref=con.at[pl.ds(block_at(r), rows), :],
            dst_ref=columns.at[r - 1],
            send_sem=col_send.at[t, r - 1],
            recv_sem=col_recv.at[t, r - 1],
            device_id={"expert": peer(r, 0)},
            device_id_type=MESH,
        )

    def line_sum(t, r):
        con, pairs, lines = sums[t][:3]
        at = pl.ds(block_at(r), rows)
        inner = pl.ds(pl.multiple_of(lax.rem(p + r, SIDE) * rows, rows), rows)
        total = con[at, :].astype(F32) + pairs[at, :].astype(F32)
        for k in range(SIDE - 1):
            total = total + lines[k, inner, :].astype(F32)
        return total

    def send_blocks(t):
        con = sums[t][0]
        pair(t, 0).wait_recv()
        for r in range(1, SIDE):
            to_line(t, r).wait_recv()
        for r in (2, 1, 3):
            con[pl.ds(block_at(r), rows), :] = line_sum(t, r).astype(BF16)
            to_block(t, r).start()

    def finish(t):
        columns, out = sums[t][3:]
        total = line_sum(t, 0)
        for r in range(1, SIDE):
            to_block(t, r).wait_recv()
            total = total + columns[r - 1].astype(F32)
        out[...] = total.astype(BF16)

    lax.fori_loop(0, 2, outputs, 0)
    lax.fori_loop(tiles, 2 * tiles, unpack(outs, con_m), 0)
    send_pairs(0)
    begin(10, -10, 6, -6)
    lax.fori_loop(0, 2, backward, 0)
    lax.fori_loop(tiles, 2 * tiles, unpack(back, con_t), 0)
    send_pairs(1)
    relay(14, -14, 12, -12)
    begin(5, -5, 1, -1)
    lax.fori_loop(0, tiles, unpack(outs, con_m), 0)
    send_lines(0)
    lax.fori_loop(0, tiles, unpack(back, con_t), 0)
    relay(13, -13)
    relay(9, -9, 7, -7)
    send_lines(1)
    relay(4, -4, 2, -2)
    send_blocks(0)
    relay(8, -8)
    send_blocks(1)
    finish(0)
    relay(3, -3)
    finish(1)
    total = add_up(0)
    for i in range(2):
        down_ref[i] = total[:, i * hid : (i + 1) * hid]

    for t in range(2):
        for rp in range(SIDE):
            for rq in range(SIDE):
                cross(t, rp, rq).wait_send()
                if rp or rq:
                    gather(t, rp, rq).wait_send()
        for r in range(SIDE):
            pair(t, r).wait_send()
        for r in range(1, SIDE):
            to_line(t, r).wait_send()
            to_block(t, r).wait_send()
    for far in NEXT:
        travel(far).wait_send()


def hand_over(*refs):
    n = len(refs) // 2
    for k in range(n):
        refs[n + k][...] = refs[k][...]


def on_device(n_dp, tokens, expert_ids, gate_probs, w_gate, w_up, w_down, out_grad):
    rows, width = tokens.shape
    mine, _, hid = w_gate.shape
    half = CHIPS * rows
    share = width // n_dp
    taken = 2 * CHIPS * CAP
    vmem = pl.BlockSpec(memory_space=pltpu.VMEM)
    hbm = pl.BlockSpec(memory_space=pltpu.HBM)
    dma = pltpu.SemaphoreType.DMA
    reach = SIDE - 1
    mixed, token_grad, down = pl.pallas_call(
        lambda *refs: layer_kernel(n_dp, *refs),
        out_shape=(
            jax.ShapeDtypeStruct((rows, width), BF16),
            jax.ShapeDtypeStruct((rows, width), BF16),
            jax.ShapeDtypeStruct((mine, share, hid), F32),
        ),
        in_specs=[hbm] * 7,
        out_specs=(vmem, vmem, vmem),
        scratch_shapes=[
            pltpu.VMEM(expert_ids.shape[::-1], jnp.int32),
            pltpu.VMEM(gate_probs.shape[::-1], F32),
            pltpu.VMEM((2 * half, width + 256), BF16),
            pltpu.VMEM((2 * half, width), BF16),
            pltpu.VMEM((mine, width, hid), BF16),
            pltpu.VMEM((mine, width, hid), BF16),
            pltpu.VMEM((mine, hid, width), BF16),
            pltpu.VMEM((2 * half, 2 * TILE // rows * CAP), BF16),
            pltpu.VMEM((mine, taken, width + 128), BF16),
            pltpu.VMEM((mine, taken, width), BF16),
            pltpu.VMEM((mine, taken, hid), F32),
            pltpu.VMEM((mine, taken, hid), F32),
            pltpu.VMEM((mine, taken, hid), BF16),
            pltpu.VMEM((mine, taken, width), BF16),
            pltpu.VMEM((mine, taken, width), BF16),
            pltpu.VMEM((2 * half, width), BF16),
            pltpu.VMEM((2 * half, width), BF16),
            pltpu.VMEM((half, width), BF16),
            pltpu.VMEM((half, width), BF16),
            pltpu.VMEM((reach, SIDE * rows, width), BF16),
            pltpu.VMEM((reach, SIDE * rows, width), BF16),
            pltpu.VMEM((reach, rows, width), BF16),
            pltpu.VMEM((reach, rows, width), BF16),
            pltpu.VMEM((width, mine * hid), BF16),
            pltpu.VMEM((len(NEXT), share, mine * hid), BF16),
            dma((4,)),
            dma((3,)),
            dma((2, SIDE, SIDE)),
            dma((2, SIDE, SIDE)),
            dma((2, SIDE, SIDE)),
            dma((2, SIDE, SIDE)),
            dma((2, SIDE)),
            dma((2, SIDE)),
            dma((2, reach)),
            dma((2, reach)),
            dma((2, reach)),
            dma((2, reach)),
            dma((len(NEXT),)),
            dma((len(NEXT),)),
        ],
        compiler_params=pltpu.CompilerParams(
            collective_id=0, has_side_effects=True, vmem_limit_bytes=58 * 1024 * 1024
        ),
    )(tokens, expert_ids.T, gate_probs.T, w_gate, w_up, w_down, out_grad)
    results = (mixed, token_grad, down)
    mixed, token_grad, down = pl.pallas_call(
        hand_over,
        out_shape=tuple(jax.ShapeDtypeStruct(part.shape, part.dtype) for part in results),
        in_specs=[vmem] * 3,
        out_specs=(vmem,) * 3,
        compiler_params=pltpu.CompilerParams(vmem_limit_bytes=58 * 1024 * 1024),
    )(*results)
    return mixed, token_grad, jnp.transpose(down, (0, 2, 1))


def solution(mesh):
    n_dp = mesh.shape["dp"]

    def body(*args):
        return on_device(n_dp, *args)

    return jax.shard_map(
        body,
        mesh=mesh,
        in_specs=(
            P(("expert", "dp"), None),
            P(("expert", "dp"), None),
            P(("expert", "dp"), None),
            P("expert", None, None),
            P("expert", None, None),
            P("expert", None, None),
            P(("expert", "dp"), None),
        ),
        out_specs=(P(("expert", "dp"), None), P(("expert", "dp"), None), P("expert", None, "dp")),
        check_vma=False,
    )
```

```python
import jax
import jax.numpy as jnp
from jax import lax
from jax.experimental import pallas as pl
from jax.experimental.pallas import tpu as pltpu
from jax.sharding import PartitionSpec as P

MESH = pl.DeviceIdType.MESH
F32 = jnp.float32
BF16 = jnp.bfloat16
SIDE = 4
CHIPS = SIDE * SIDE
TILE = 256
CAP = 8

PARENT = {1: 2, 2: 3, 3: 0, 4: 3, 5: 4, 6: 7, 7: 8, 8: 3, 9: 8, 10: 9, 11: 12, 12: 13, 13: 8, 14: 13, 15: 14, 16: 14}
NEXT = dict(PARENT)
NEXT.update({-far: -near for far, near in PARENT.items() if far < 16})
FROM = {near: [far for far in NEXT if NEXT[far] == near] for near in set(NEXT.values())}


def dot(a, b):
    return lax.dot_general(a, b, (((1,), (0,)), ((), ())), preferred_element_type=F32)


def dot_nt(a, b):
    return lax.dot_general(a, b, (((1,), (1,)), ((), ())), preferred_element_type=F32)


def dot_tn(a, b):
    return lax.dot_general(a, b, (((0,), (0,)), ((), ())), preferred_element_type=F32)


def layer_kernel(
    n_dp,
    tok_hbm, ids_hbm, prob_hbm, wg_hbm, wu_hbm, wd_hbm, grad_hbm,
    mixed_ref, tgrad_ref, down_ref,
    ids_ref, prob_ref, x_all, dy_all, wg, wu, wd, slots, xs, dys, coef_g, coef_u, ph, outs, back, con_m, con_t, pair_m, pair_t, row_m, row_t, col_m, col_t, part, ring,
    own_sem, w_sem, ag_send, ag_recv, in_send, in_recv, pair_send, pair_recv, row_send, row_recv, col_send, col_recv, z_send, z_recv,
):
    e = lax.axis_index("expert")
    z = lax.axis_index("dp")
    rows, width = tok_hbm.shape
    half = CHIPS * rows
    hid = wg_hbm.shape[2]
    share = width // n_dp
    c = lax.rem(e, 2)
    x = lax.rem(lax.div(e, 2), SIDE)
    y = lax.div(e, 2 * SIDE)
    p = x + c * (y - x)
    q = y + c * (x - y)
    other = e + 1 - 2 * c

    def peer(dp, dq):
        p2, q2 = lax.rem(p + dp, SIDE), lax.rem(q + dq, SIDE)
        x2, y2 = p2 + c * (q2 - p2), q2 + c * (p2 - q2)
        return (y2 * SIDE + x2) * 2 + c

    def block(rp, rq):
        slot = lax.rem(q + SIDE - rq, SIDE) * SIDE + lax.rem(p + SIDE - rp, SIDE)
        return pl.multiple_of(slot * rows, rows)

    mine = block(0, 0)
    own = [
        pltpu.make_async_copy(ids_hbm, ids_ref, own_sem.at[0]),
        pltpu.make_async_copy(prob_hbm, prob_ref, own_sem.at[1]),
        pltpu.make_async_copy(tok_hbm, x_all.at[pl.ds(mine, rows), :width], own_sem.at[2]),
        pltpu.make_async_copy(grad_hbm, dy_all.at[pl.ds(mine, rows), :], own_sem.at[3]),
    ]
    for load in own:
        load.start()

    loads = []
    for k, (src, dst) in enumerate(((wg_hbm, wg), (wu_hbm, wu), (wd_hbm, wd))):
        load = pltpu.make_async_copy(src, dst, w_sem.at[k])
        load.start()
        loads.append(load)

    barrier = pltpu.get_barrier_semaphore()
    near = [{"expert": other}]
    for r in range(1, SIDE):
        near.append({"expert": peer(r, 0)})
        near.append({"expert": peer(0, r)})
    reach = sorted({NEXT[far] - far for far in NEXT})
    for r in reach:
        near.append({"dp": lax.rem(z + n_dp - r, n_dp)})
    for device in near:
        pl.semaphore_signal(barrier, inc=1, device_id=device, device_id_type=MESH)

    lanes = 128
    experts = 64
    gate_at, code_at = width, width + lanes
    expert_of = lax.broadcasted_iota(jnp.int32, (experts, rows), 0)
    own[0].wait()
    own[1].wait()
    gates = jnp.zeros((experts, rows), F32)
    taken = jnp.zeros((experts, rows), F32)
    for k in range(ids_ref.shape[0]):
        hit = ids_ref[k : k + 1, :] == expert_of
        gates = gates + jnp.where(hit, prob_ref[k : k + 1, :], 0.0)
        taken = taken + jnp.where(hit, 1.0, 0.0)
    high = gates.astype(BF16)
    low = (gates - high.astype(F32)).astype(BF16)
    before = lax.broadcasted_iota(jnp.int32, (rows, rows), 0) < lax.broadcasted_iota(jnp.int32, (rows, rows), 1)
    rank = dot(taken.astype(BF16), before.astype(F32).astype(BF16))
    code = (taken * (rank + 1.0) - 1.0).astype(BF16)
    line = lax.broadcasted_iota(jnp.int32, (experts, lanes), 0)
    lane = lax.broadcasted_iota(jnp.int32, (experts, lanes), 1)
    first = (line == lane).astype(F32).astype(BF16)
    second = (line + experts == lane).astype(F32).astype(BF16)
    x_all[pl.ds(mine, rows), gate_at:code_at] = (dot_tn(high, first) + dot_tn(low, second)).astype(BF16)
    x_all[pl.ds(mine, rows), code_at:] = dot_tn(code, first).astype(BF16)
    own[2].wait()
    own[3].wait()

    arrays = (x_all, dy_all)

    def gather(t, rp, rq):
        at = block(0, 0) if rq == 0 else block(rp, 0)
        ref = arrays[t].at[pl.ds(at, rows), :]
        return pltpu.make_async_remote_copy(
            src_ref=ref,
            dst_ref=ref,
            send_sem=ag_send.at[t, rp, rq],
            recv_sem=ag_recv.at[t, rp, rq],
            device_id={"expert": peer(rp, 0) if rq == 0 else peer(0, rq)},
            device_id_type=MESH,
        )

    def cross(t, rp, rq):
        at = block(rp, rq)
        return pltpu.make_async_remote_copy(
            src_ref=arrays[t].at[pl.ds(at, rows), :],
            dst_ref=arrays[t].at[pl.ds(pl.multiple_of(half + at, rows), rows), :],
            send_sem=in_send.at[t, rp, rq],
            recv_sem=in_recv.at[t, rp, rq],
            device_id={"expert": other},
            device_id_type=MESH,
        )

    pl.semaphore_wait(barrier, len(near))

    for t in range(2):
        for r in range(1, SIDE):
            gather(t, r, 0).start()
        for r in range(1, SIDE):
            gather(t, 0, r).start()
        cross(t, 0, 0).start()
    for t in range(2):
        for rp in (1, 3, 2):
            gather(t, rp, 0).wait_recv()
            for rq in range(1, SIDE):
                gather(t, rp, rq).start()
            cross(t, rp, 0).start()

    def pass_on(t):
        for rp in range(SIDE):
            for rq in range(1, SIDE):
                gather(t, rp, rq).wait_recv()
                cross(t, rp, rq).start()

    per = TILE // rows * CAP
    line = lax.broadcasted_iota(jnp.int32, (lanes, 2 * per), 0)
    lane = lax.broadcasted_iota(jnp.int32, (lanes, 2 * per), 1)
    pick_code = (line == jnp.where(lane >= per, 2 * e + 1, 2 * e)).astype(F32).astype(BF16)
    token = lax.broadcasted_iota(jnp.int32, (TILE, 2 * per), 0)
    place = lax.broadcasted_iota(jnp.int32, (TILE, 2 * per), 1)
    place = jnp.where(place >= per, place - per, place)
    same = jnp.where((token >> 5) == (place >> 3), 1.0, 0.0)
    wanted = (place & (CAP - 1)).astype(F32)

    def tile_at(i):
        return pl.ds(pl.multiple_of(i * TILE, TILE), TILE)

    def rows_at(i):
        return pl.ds(pl.multiple_of(i * per, per), per)

    def pack_x(i, carry):
        at = tile_at(i)
        codes = dot(x_all[at, code_at:], pick_code)
        chosen = (jnp.where(codes == wanted, 1.0, 0.0) * same).astype(BF16)
        slots[at, :] = chosen
        got = dot_tn(chosen, x_all[at, :code_at]).astype(BF16)
        xs[0, rows_at(i), :] = got[:per]
        xs[1, rows_at(i), :] = got[per:]
        return carry

    def pack_dy(i, carry):
        got = dot_tn(slots[tile_at(i), :], dy_all[tile_at(i), :]).astype(BF16)
        dys[0, rows_at(i), :] = got[:per]
        dys[1, rows_at(i), :] = got[per:]
        return carry

    gate_line = lax.broadcasted_iota(jnp.int32, (lanes, hid), 0)
    gate_line = jnp.where(gate_line >= experts, gate_line - experts, gate_line)

    def forward(k, carry):
        gate = dot(xs[k, :, :width], wg[k])
        up = dot(xs[k, :, :width], wu[k])
        prob = dot(xs[k, :, gate_at:], (gate_line == 2 * e + k).astype(F32).astype(BF16))
        sig = jax.nn.sigmoid(gate)
        scaled = prob * (gate * sig)
        ph[k] = (scaled * up).astype(BF16)
        coef_u[k] = scaled
        coef_g[k] = prob * up * sig * (1.0 + gate * (1.0 - sig))
        return carry

    tiles = half // TILE
    pass_on(0)
    lax.fori_loop(0, tiles, pack_x, 0)
    for rp in range(SIDE):
        for rq in range(SIDE):
            cross(0, rp, rq).wait_recv()
    lax.fori_loop(tiles, 2 * tiles, pack_x, 0)
    pass_on(1)
    for load in loads:
        load.wait()
    lax.fori_loop(0, 2, forward, 0)
    lax.fori_loop(0, tiles, pack_dy, 0)
    for rp in range(SIDE):
        for rq in range(SIDE):
            cross(1, rp, rq).wait_recv()
    lax.fori_loop(tiles, 2 * tiles, pack_dy, 0)

    def partial(k):
        def one(i, carry):
            at = tile_at(i)
            part[k, at, :] = dot_tn(dys[k, :, at], ph[k]).astype(BF16)
            return carry

        return one

    slot_of = {far: k for k, far in enumerate(sorted(NEXT))}

    def owned(far):
        owner = lax.rem(z + n_dp - far, n_dp)
        return pl.ds(pl.multiple_of(owner * share, share), share)

    def travel(far, k):
        src = ring.at[slot_of[FROM[far][0]], k] if far in FROM else part.at[k, owned(far), :]
        return pltpu.make_async_remote_copy(
            src_ref=src,
            dst_ref=ring.at[slot_of[far], k],
            send_sem=z_send.at[slot_of[far], k],
            recv_sem=z_recv.at[slot_of[far], k],
            device_id={"dp": lax.rem(z + n_dp + NEXT[far] - far, n_dp)},
            device_id_type=MESH,
        )

    def add_up(far, k):
        total = part[k, owned(far), :].astype(F32)
        for child in FROM[far]:
            travel(child, k).wait_recv()
            total = total + ring[slot_of[child], k, :, :].astype(F32)
        return total

    def relay(*fars):
        for k in range(2):
            for far in fars:
                ring[slot_of[FROM[far][0]], k, :, :] = add_up(far, k).astype(BF16)
                travel(far, k).start()

    def begin(*fars):
        for k in range(2):
            for far in fars:
                travel(far, k).start()

    for k in range(2):
        lax.fori_loop(0, width // TILE, partial(k), 0)
        for far in (16, 15, -15, 11, -11):
            travel(far, k).start()

    def outputs(k, carry):
        outs[k] = dot(ph[k], wd[k]).astype(BF16)
        return carry

    def backward(k, carry):
        hidden_grad = dot_nt(dys[k], wd[k])
        gate_grad = (hidden_grad * coef_g[k]).astype(BF16)
        up_grad = (hidden_grad * coef_u[k]).astype(BF16)
        back[k] = (dot_nt(gate_grad, wg[k]) + dot_nt(up_grad, wu[k])).astype(BF16)
        return carry

    def unpack(source, con):
        def one(i, carry):
            both = jnp.concatenate([source[0, rows_at(i), :], source[1, rows_at(i), :]], axis=0)
            con[tile_at(i), :] = dot(slots[tile_at(i), :], both).astype(BF16)
            return carry

        return one

    sums = ((con_m, pair_m, row_m, col_m, mixed_ref), (con_t, pair_t, row_t, col_t, tgrad_ref))

    def pair(t, r):
        con, pairs = sums[t][:2]
        at = lax.rem(p + r, SIDE) * (SIDE * rows)
        return pltpu.make_async_remote_copy(
            src_ref=con.at[pl.ds(pl.multiple_of(half + at, SIDE * rows), SIDE * rows), :],
            dst_ref=pairs.at[pl.ds(pl.multiple_of(at, SIDE * rows), SIDE * rows), :],
            send_sem=pair_send.at[t, r],
            recv_sem=pair_recv.at[t, r],
            device_id={"expert": other},
            device_id_type=MESH,
        )

    def send_pairs(t):
        for r in (2, 1, 3, 0):
            pair(t, r).start()

    def line_at(rq):
        return pl.ds(pl.multiple_of(lax.rem(q + rq, SIDE) * (SIDE * rows), SIDE * rows), SIDE * rows)

    def to_line(t, r):
        con, _, lines = sums[t][:3]
        return pltpu.make_async_remote_copy(
            src_ref=con.at[line_at(r), :],
            dst_ref=lines.at[r - 1],
            send_sem=row_send.at[t, r - 1],
            recv_sem=row_recv.at[t, r - 1],
            device_id={"expert": peer(0, r)},
            device_id_type=MESH,
        )

    def send_lines(t):
        con, pairs = sums[t][:2]
        for r in (2, 1, 3):
            at = line_at(r)
            pair(t, r).wait_recv()
            con[at, :] = (con[at, :].astype(F32) + pairs[at, :].astype(F32)).astype(BF16)
            to_line(t, r).start()

    def block_at(r):
        return pl.multiple_of(lax.rem(q, SIDE) * (SIDE * rows) + lax.rem(p + r, SIDE) * rows, rows)

    def to_block(t, r):
        con, columns = sums[t][0], sums[t][3]
        return pltpu.make_async_remote_copy(
            src_ref=con.at[pl.ds(block_at(r), rows), :],
            dst_ref=columns.at[r - 1],
            send_sem=col_send.at[t, r - 1],
            recv_sem=col_recv.at[t, r - 1],
            device_id={"expert": peer(r, 0)},
            device_id_type=MESH,
        )

    def line_sum(t, r):
        con, pairs, lines = sums[t][:3]
        at = pl.ds(block_at(r), rows)
        inner = pl.ds(pl.multiple_of(lax.rem(p + r, SIDE) * rows, rows), rows)
        total = con[at, :].astype(F32) + pairs[at, :].astype(F32)
        for k in range(SIDE - 1):
            total = total + lines[k, inner, :].astype(F32)
        return total

    def send_blocks(t):
        con = sums[t][0]
        pair(t, 0).wait_recv()
        for r in range(1, SIDE):
            to_line(t, r).wait_recv()
        for r in (2, 1, 3):
            con[pl.ds(block_at(r), rows), :] = line_sum(t, r).astype(BF16)
            to_block(t, r).start()

    def finish(t):
        columns, out = sums[t][3:]
        total = line_sum(t, 0)
        for r in range(1, SIDE):
            to_block(t, r).wait_recv()
            total = total + columns[r - 1].astype(F32)
        out[...] = total.astype(BF16)

    lax.fori_loop(0, 2, outputs, 0)
    lax.fori_loop(tiles, 2 * tiles, unpack(outs, con_m), 0)
    send_pairs(0)
    begin(10, -10, 6, -6)
    lax.fori_loop(0, 2, backward, 0)
    lax.fori_loop(tiles, 2 * tiles, unpack(back, con_t), 0)
    send_pairs(1)
    relay(14, -14, 12, -12)
    begin(5, -5, 1, -1)
    lax.fori_loop(0, tiles, unpack(outs, con_m), 0)
    send_lines(0)
    lax.fori_loop(0, tiles, unpack(back, con_t), 0)
    relay(13, -13)
    relay(9, -9, 7, -7)
    send_lines(1)
    relay(4, -4, 2, -2)
    send_blocks(0)
    relay(8, -8)
    send_blocks(1)
    finish(0)
    relay(3, -3)
    finish(1)
    for k in range(2):
        down_ref[k] = add_up(0, k)

    for t in range(2):
        for rp in range(SIDE):
            for rq in range(SIDE):
                cross(t, rp, rq).wait_send()
                if rp or rq:
                    gather(t, rp, rq).wait_send()
        for r in range(SIDE):
            pair(t, r).wait_send()
        for r in range(1, SIDE):
            to_line(t, r).wait_send()
            to_block(t, r).wait_send()
    for far in NEXT:
        travel(far, 0).wait_send()
        travel(far, 1).wait_send()


def hand_over(*refs):
    n = len(refs) // 2
    for k in range(n):
        refs[n + k][...] = refs[k][...]


def on_device(n_dp, tokens, expert_ids, gate_probs, w_gate, w_up, w_down, out_grad):
    rows, width = tokens.shape
    mine, _, hid = w_gate.shape
    half = CHIPS * rows
    share = width // n_dp
    taken = 2 * CHIPS * CAP
    vmem = pl.BlockSpec(memory_space=pltpu.VMEM)
    hbm = pl.BlockSpec(memory_space=pltpu.HBM)
    dma = pltpu.SemaphoreType.DMA
    reach = SIDE - 1
    mixed, token_grad, down = pl.pallas_call(
        lambda *refs: layer_kernel(n_dp, *refs),
        out_shape=(
            jax.ShapeDtypeStruct((rows, width), BF16),
            jax.ShapeDtypeStruct((rows, width), BF16),
            jax.ShapeDtypeStruct((mine, share, hid), F32),
        ),
        in_specs=[hbm] * 7,
        out_specs=(vmem, vmem, vmem),
        scratch_shapes=[
            pltpu.VMEM(expert_ids.shape[::-1], jnp.int32),
            pltpu.VMEM(gate_probs.shape[::-1], F32),
            pltpu.VMEM((2 * half, width + 256), BF16),
            pltpu.VMEM((2 * half, width), BF16),
            pltpu.VMEM((mine, width, hid), BF16),
            pltpu.VMEM((mine, width, hid), BF16),
            pltpu.VMEM((mine, hid, width), BF16),
            pltpu.VMEM((2 * half, 2 * TILE // rows * CAP), BF16),
            pltpu.VMEM((mine, taken, width + 128), BF16),
            pltpu.VMEM((mine, taken, width), BF16),
            pltpu.VMEM((mine, taken, hid), F32),
            pltpu.VMEM((mine, taken, hid), F32),
            pltpu.VMEM((mine, taken, hid), BF16),
            pltpu.VMEM((mine, taken, width), BF16),
            pltpu.VMEM((mine, taken, width), BF16),
            pltpu.VMEM((2 * half, width), BF16),
            pltpu.VMEM((2 * half, width), BF16),
            pltpu.VMEM((half, width), BF16),
            pltpu.VMEM((half, width), BF16),
            pltpu.VMEM((reach, SIDE * rows, width), BF16),
            pltpu.VMEM((reach, SIDE * rows, width), BF16),
            pltpu.VMEM((reach, rows, width), BF16),
            pltpu.VMEM((reach, rows, width), BF16),
            pltpu.VMEM((mine, width, hid), BF16),
            pltpu.VMEM((len(NEXT), mine, share, hid), BF16),
            dma((4,)),
            dma((3,)),
            dma((2, SIDE, SIDE)),
            dma((2, SIDE, SIDE)),
            dma((2, SIDE, SIDE)),
            dma((2, SIDE, SIDE)),
            dma((2, SIDE)),
            dma((2, SIDE)),
            dma((2, reach)),
            dma((2, reach)),
            dma((2, reach)),
            dma((2, reach)),
            dma((len(NEXT), mine)),
            dma((len(NEXT), mine)),
        ],
        compiler_params=pltpu.CompilerParams(
            collective_id=0, has_side_effects=True, vmem_limit_bytes=58 * 1024 * 1024
        ),
    )(tokens, expert_ids.T, gate_probs.T, w_gate, w_up, w_down, out_grad)
    results = (mixed, token_grad, down)
    mixed, token_grad, down = pl.pallas_call(
        hand_over,
        out_shape=tuple(jax.ShapeDtypeStruct(part.shape, part.dtype) for part in results),
        in_specs=[vmem] * 3,
        out_specs=(vmem,) * 3,
        compiler_params=pltpu.CompilerParams(vmem_limit_bytes=58 * 1024 * 1024),
    )(*results)
    return mixed, token_grad, jnp.transpose(down, (0, 2, 1))


def solution(mesh):
    n_dp = mesh.shape["dp"]

    def body(*args):
        return on_device(n_dp, *args)

    return jax.shard_map(
        body,
        mesh=mesh,
        in_specs=(
            P(("expert", "dp"), None),
            P(("expert", "dp"), None),
            P(("expert", "dp"), None),
            P("expert", None, None),
            P("expert", None, None),
            P("expert", None, None),
            P(("expert", "dp"), None),
        ),
        out_specs=(P(("expert", "dp"), None), P(("expert", "dp"), None), P("expert", None, "dp")),
        check_vma=False,
    )
```
